256 devices in a mesh: src: 64 (over x, y, z_hi), blk: 4 (over z_lo, core).
Axes of the slice: x: 4, y: 4, z: 8 (z_hi: 4, z_lo: 2; z = z_hi * 2 + z_lo), core: 2. Of those that a mesh axis runs over, the one named last changes fastest.
Arguments:
- sources: bfloat16 [524288, 1024], P(('src', 'blk')), may hold values from -18 to 18
- targets: bfloat16 [1024, 1024], P('blk'), may hold values from -6 to 6
- log_src: float32 [524288], P(('src', 'blk')), may hold values from -1 to 2.1
- log_tgt: float32 [1024], P('blk'), may hold values from -1 to 1
- potential: float32 [1024], P('blk'), may hold values from -60 to 60
Outputs:
- source_potential: float32 [524288], P(('src', 'blk'))
- target_potential: float32 [1024], P('blk')
The draws below stay inside these ranges and needn't reach their ends.
All inputs are finite; a program needn't handle non-finite values.
Results may differ from the reference program's by a relative error of at most 0.0003.
Values may be sent and summed in bfloat16 or wider, within the bound.
A program may use at most 64 MiB of HBM per device.

```python
import math
import jax
import jax.numpy as jnp
from jax import lax

D = 1024
ROWS_DEV = 2048
NS = 524288
NT = 1024


def target_base(key):
    return jnp.clip(jax.random.normal(key, (NT, D), jnp.float32), -6.0, 6.0)


def draw_targets(key, part):
    base = target_base(key)
    return base.astype(jnp.bfloat16)


def draw_sources(key, part):
    key = jax.random.fold_in(key, 7)
    values = jnp.clip(jax.random.normal(key, (NS, D), jnp.float32), -6.0, 6.0)
    return values.astype(jnp.bfloat16)


def draw_log_src(key, part):
    key = jax.random.fold_in(key, 11)
    positions = jnp.arange(NS).astype(jnp.float32)
    rising = jnp.log(1.0 + 2.0 * positions / max(NS - 1, 1))
    noise = jax.random.uniform(key, (NS,), jnp.float32, -0.5, 0.5)
    return rising + noise


def draw_potential(key, part):
    key = jax.random.fold_in(key, 13)
    values = jax.random.uniform(key, (NT,), jnp.float32, -2.0, 2.0)
    return values


def block_levels(key, extent, shards, low, largest):
    level, own = 1.0, jax.random.fold_in(key, 6)
    for axis_at, blocks in shards:
        heights = jnp.exp(jax.random.uniform(jax.random.fold_in(own, axis_at), (blocks,), jnp.float32, low / len(shards), largest / len(shards)))
        level = level * jnp.repeat(heights, extent[axis_at] // blocks).reshape([-1 if axis == axis_at else 1 for axis in range(len(extent))])
    return level


def setup_inputs(seed: int = 0) -> dict:
    seeds = jax.random.split(jax.random.key(seed), 6)
    sources = draw_sources(jax.random.fold_in(seeds[5], 71), 0)
    targets = draw_targets(jax.random.fold_in(seeds[5], 71), 0)
    log_src = draw_log_src(jax.random.fold_in(seeds[5], 71), 0)
    log_tgt = jnp.clip(jax.random.uniform(seeds[3], (NT,), jnp.float32, -1.0, 1.0) * block_levels(seeds[3], (NT,), ((0, 4),), -0.4, 0.0), -1.0, 1.0)
    potential = draw_potential(jax.random.fold_in(seeds[5], 71), 0)
    return dict(sources=sources, targets=targets, log_src=log_src, log_tgt=log_tgt, potential=potential)


EPSILON = 0.5

def cost_block(rows, targets, tgt_norms):
    src_norms = lax.optimization_barrier(jnp.sum(jnp.square(rows.astype(jnp.float32)), axis=1))
    inner = jnp.dot(rows, targets.T, preferred_element_type=jnp.float32)
    return (src_norms[:, None] + tgt_norms[None, :] - 2.0 * inner) / math.sqrt(D) - 2.0 * math.sqrt(D)

def reference(sources, targets, log_src, log_tgt, potential):
    tgt_norms = lax.optimization_barrier(jnp.sum(jnp.square(targets.astype(jnp.float32)), axis=1))
    bias = log_tgt + potential / EPSILON

    def sweep(carry, inputs):
        rows, weights = inputs
        run_max, run_sum = carry
        cost = cost_block(rows, targets, tgt_norms)
        scores = bias[None, :] - cost / EPSILON
        top = lax.optimization_barrier(jnp.max(scores, axis=1))
        src_pot = -EPSILON * (top + jnp.log(lax.optimization_barrier(jnp.sum(jnp.exp(scores - top[:, None]), axis=1))))
        col_scores = weights[:, None] + (src_pot[:, None] - cost) / EPSILON
        col_top = lax.optimization_barrier(jnp.max(col_scores, axis=0))
        col_total = lax.optimization_barrier(jnp.sum(jnp.exp(col_scores - col_top[None, :]), axis=0))
        merged = jnp.maximum(run_max, col_top)
        new_sum = run_sum * jnp.exp(run_max - merged) + col_total * jnp.exp(col_top - merged)
        return ((merged, new_sum), src_pot)
    blocks = NS // ROWS_DEV
    start = (jnp.full((NT,), -1e+30, jnp.float32), jnp.zeros((NT,), jnp.float32))
    (run_max, run_sum), pots = lax.scan(sweep, start, (sources.reshape(blocks, ROWS_DEV, D), log_src.reshape(blocks, ROWS_DEV)))
    target_potential = -EPSILON * (run_max + jnp.log(run_sum))
    return (pots.reshape(NS), target_potential)
```

```python
import functools
import math

import jax
import jax.numpy as jnp
from jax import lax
from jax.experimental import pallas as pl
from jax.experimental.pallas import tpu as pltpu
from jax.sharding import PartitionSpec as P

MESH = pl.DeviceIdType.MESH
LOG2E = math.log2(math.e)
LN2 = math.log(2.0)
F32 = jnp.float32

ROWS = 2048
COLS = 1024
BLOCK = 256
WIDTH = 1024
TILE = 128
SIDE = 4
PIECES = 2
PART = BLOCK // 2 // PIECES


def dot_t(left, right):
    return lax.dot_general(left, right, (((1,), (1,)), ((), ())), preferred_element_type=F32)


def fold_lanes(op, value):
    while value.shape[1] > TILE:
        half = value.shape[1] // 2
        value = op(value[:, :half], value[:, half:])
    return value


def kernel(
    sources,
    targets,
    log_src,
    log_tgt,
    potential,
    src_out,
    tgt_out,
    src_v,
    near_t,
    far_t,
    bias_v,
    weight_v,
    row_bias,
    wide_bias,
    norms,
    scores,
    row_max,
    row_sum,
    shift,
    col_max,
    col_sum,
    col_log,
    line_in,
    line_out,
    plane_in,
    load_sem,
    send_sem,
    recv_sem,
    reduce_sem,
):
    src = lax.axis_index("src")
    blk = lax.axis_index("blk")
    x, y, z_hi = src // (SIDE * SIDE), (src // SIDE) % SIDE, src % SIDE
    z_lo, core = blk // 2, blk % 2
    z = z_hi * 2 + z_lo

    def device(to_x, to_y, to_z, to_core):
        return ((to_x * SIDE + to_y) * SIDE + to_z // 2, (to_z % 2) * 2 + to_core)

    def line(step, to_core):
        return device(x, y, (z + step) % (2 * SIDE), to_core)

    def plane(step, to_core):
        return device((x + step // SIDE) % SIDE, (y + step % SIDE) % SIDE, z, to_core)

    sibling = line(0, 1 - core)
    above, below = line(1, core), line(2 * SIDE - 1, core)

    loads = []

    def load(from_ref, to_ref):
        copy = pltpu.make_async_copy(from_ref, to_ref, load_sem.at[len(loads)])
        copy.start()
        loads.append(copy)
        return copy

    own_rows = pl.ds(pl.multiple_of(core * BLOCK, BLOCK), BLOCK)
    sib_rows = pl.ds(pl.multiple_of((1 - core) * BLOCK, BLOCK), BLOCK)
    load_t = load(targets, near_t.at[own_rows])
    load_p = load(potential, bias_v.at[0:2])
    load_l = load(log_tgt, bias_v.at[8:10])
    load_w = load(log_src, weight_v)
    quarter = ROWS // 4
    load_s = [
        load(sources.at[n * quarter : (n + 1) * quarter], src_v.at[n * quarter : (n + 1) * quarter])
        for n in range(4)
    ]

    barrier = pltpu.get_barrier_semaphore()

    def greet(peers):
        for peer in peers:
            pl.semaphore_signal(barrier, inc=1, device_id=peer, device_id_type=MESH)
        pl.semaphore_wait(barrier, len(peers))

    @pl.when(core == 0)
    def _():
        greet(
            [sibling, above, below]
            + [line(step, 1) for step in range(1, 2 * SIDE)]
            + [plane(step, 1) for step in range(1, SIDE * SIDE)]
        )

    @pl.when(core == 1)
    def _():
        greet(
            [sibling]
            + [line(step, to) for step in range(1, 2 * SIDE) for to in range(2)]
            + [plane(step, to) for step in range(1, SIDE * SIDE) for to in range(2)]
        )

    sends = []

    def send(from_ref, to_ref, number, peer):
        copy = pltpu.make_async_remote_copy(
            src_ref=from_ref,
            dst_ref=to_ref,
            send_sem=send_sem.at[number],
            recv_sem=recv_sem.at[number],
            device_id=peer,
            device_id_type=MESH,
        )
        copy.start()
        sends.append(copy)
        return copy

    load_t.wait()
    core_rows = core * BLOCK
    up, down, pass_up, pass_down = [], [], [], []
    for piece in range(PIECES):
        low = pl.ds(pl.multiple_of(core_rows + piece * PART, PART), PART)
        high = pl.ds(pl.multiple_of(core_rows + BLOCK // 2 + piece * PART, PART), PART)
        land_low = pl.ds(pl.multiple_of(core * 2 * PART, PART), PART)
        land_high = pl.ds(pl.multiple_of(core * 2 * PART + PART, PART), PART)
        up.append(send(near_t.at[low], far_t.at[piece, land_low], 4 * piece, above))
        down.append(send(near_t.at[high], far_t.at[piece, land_high], 4 * piece + 1, below))
    near = send(near_t.at[own_rows], near_t.at[own_rows], 4 * PIECES, sibling)

    load_p.wait()
    load_l.wait()
    for half in range(2):
        rows = pl.ds(pl.multiple_of(core_rows + half * TILE, TILE), TILE)
        block = near_t[rows, :].astype(F32)
        tgt_norms = jnp.sum(fold_lanes(jnp.add, block * block).T, axis=0, keepdims=True)
        bias = bias_v[8 + half : 9 + half, :] + 2.0 * bias_v[half : half + 1, :]
        row_bias[pl.ds(core * 2 + half, 1), :] = (bias - tgt_norms / 16.0) * LOG2E
    own_bias = row_bias.at[pl.ds(core * 2, 2)]
    far_bias = row_bias.at[pl.ds(4 + core * 2, 2)]
    bias_near = send(own_bias, own_bias, 4 * PIECES + 1, sibling)
    bias_far = send(own_bias, far_bias, 4 * PIECES + 2, above)

    def widen(slot):
        for half in range(2):
            row = jnp.broadcast_to(row_bias[pl.ds(slot * 2 + half, 1), :], (TILE, TILE))
            wide_bias[pl.ds(pl.multiple_of(slot * BLOCK + half * TILE, TILE), TILE), :] = row.T

    def row_pass(moving, segments, number, waits=()):
        bias = [wide_bias[rows, :] for rows in segments]
        bias = bias[0] if len(bias) == 1 else jnp.concatenate(bias, axis=0)
        length = bias.shape[0] // len(segments)
        for part in range(4):
            if waits:
                waits[part].wait()
            inner = dot_t(moving, src_v[part * quarter : (part + 1) * quarter, :])
            for tile in range(quarter // TILE):
                lanes = pl.ds(part * quarter + tile * TILE, TILE)
                value = inner[:, tile * TILE : (tile + 1) * TILE] * (LOG2E / 8.0) + bias
                for at, rows in enumerate(segments):
                    scores[rows, lanes] = value[at * length : (at + 1) * length, :]
                deep = value.reshape(-1, 8, TILE)
                top = jnp.max(deep, axis=0)
                row_max[number * 8 : number * 8 + 8, lanes] = top
                row_sum[number * 8 : number * 8 + 8, lanes] = jnp.sum(jnp.exp2(deep - top[None]), axis=0)

    widen(core)
    row_pass(near_t[own_rows, :], [own_rows], 0, load_s)
    near.wait_recv()
    bias_near.wait_recv()
    widen(1 - core)
    row_pass(near_t[sib_rows, :], [sib_rows], 1)

    bias_far.wait_recv()
    bias_pass = send(far_bias, far_bias, 4 * PIECES + 3, sibling)
    for piece in range(PIECES):
        up[piece].wait_recv()
        down[piece].wait_recv()
        land = far_t.at[piece, pl.ds(pl.multiple_of(core * 2 * PART, 2 * PART), 2 * PART)]
        passed = send(land, land, 4 * piece + 2, sibling)
        if piece == 0:
            for tile in range(ROWS // TILE):
                block = src_v[tile * TILE : (tile + 1) * TILE, :].astype(F32)
                norms[tile : tile + 1, :] = jnp.sum(fold_lanes(jnp.add, block * block).T, axis=0, keepdims=True)
            bias_pass.wait_recv()
            widen(2)
            widen(3)
        passed.wait_recv()
        segments = [
            pl.ds(2 * BLOCK + of_core * BLOCK + half * (BLOCK // 2) + piece * PART, PART)
            for of_core in range(2)
            for half in range(2)
        ]
        row_pass(far_t[piece], segments, 2 + piece)

    load_w.wait()
    peaks = row_max[...].reshape(2 + PIECES, 8, ROWS)
    peak = jnp.max(peaks, axis=0)
    total = jnp.sum(row_sum[...].reshape(2 + PIECES, 8, ROWS) * jnp.exp2(peaks - peak[None]), axis=0)
    top = jnp.max(peak, axis=0, keepdims=True)
    row_log = top + jnp.log2(jnp.sum(total * jnp.exp2(peak - top), axis=0, keepdims=True))
    weights = jnp.concatenate([weight_v[n : n + 1, :] for n in range(ROWS // TILE)], axis=1)
    shift[...] = jnp.broadcast_to(weights * LOG2E - row_log, (8, ROWS))
    for tile in range(ROWS // TILE):
        src_out[tile : tile + 1, :] = (
            norms[tile : tile + 1, :] / 32.0 - 64.0 - (0.5 * LN2) * row_log[:, tile * TILE : (tile + 1) * TILE]
        )

    for block in range(COLS // TILE):
        for group in range(TILE // 8):
            rows = pl.ds(block * TILE + group * 8, 8)
            value = scores[rows, :] + shift[...]
            peak = fold_lanes(jnp.maximum, value)
            deep = jnp.concatenate([peak] * (ROWS // TILE), axis=1)
            col_max[rows, :] = peak
            col_sum[rows, :] = fold_lanes(jnp.add, jnp.exp2(value - deep))
        rows = pl.ds(block * TILE, TILE)
        peaks = col_max[rows, :].T
        peak = jnp.max(peaks, axis=0, keepdims=True)
        total = jnp.sum(col_sum[rows, :].T * jnp.exp2(peaks - peak), axis=0, keepdims=True)
        col_log[block : block + 1, :] = peak + jnp.log2(total)

    def reduce_send(from_ref, to_ref, stage, peer):
        copy = pltpu.make_async_remote_copy(
            src_ref=from_ref,
            dst_ref=to_ref,
            send_sem=reduce_sem.at[2 * stage],
            recv_sem=reduce_sem.at[2 * stage + 1],
            device_id=peer,
            device_id_type=MESH,
        )
        copy.start()
        return copy

    def arrived(ref, stage):
        pltpu.make_async_copy(ref, ref, reduce_sem.at[2 * stage + 1]).wait()

    def left(ref, stage):
        pltpu.make_async_copy(ref, ref, reduce_sem.at[2 * stage]).wait()

    def merge(value, rows):
        deep = value.reshape(-1, 8, TILE)
        peak = jnp.max(deep, axis=0)
        total = jnp.sum(jnp.exp2(deep - peak[None]), axis=0)
        parts = [slice(n, n + rows) for n in range(0, 8, rows)]
        top = functools.reduce(jnp.maximum, [peak[p] for p in parts])
        return top + jnp.log2(sum(total[p] * jnp.exp2(peak[p] - top) for p in parts))

    for step in range(1, 2 * SIDE):
        part = col_log.at[4 * (step % 2) : 4 * (step % 2) + 4]
        slot = pl.ds(pl.multiple_of(8 * step + 4 * core, 4), 4)
        reduce_send(part, line_in.at[slot], 0, line(step, 1))

    @pl.when(core == 0)
    def _():
        reduce_send(col_log.at[0:4], line_in.at[0:4], 0, sibling)
        arrived(plane_in, 1)
        left(line_in.at[0:32], 0)

    @pl.when(core == 1)
    def _():
        line_in[4:8, :] = col_log[0:4, :]
        arrived(line_in.at[0:60], 0)
        line_out[0:4, :] = merge(line_in[...], 4)
        for step in range(1, SIDE * SIDE):
            for to in range(2):
                reduce_send(
                    line_out.at[2 * to : 2 * to + 2], plane_in.at[2 * step : 2 * step + 2], 1, plane(step, to)
                )
        reduce_send(line_out.at[0:2], plane_in.at[0:2], 1, sibling)
        plane_in[0:2, :] = line_out[2:4, :]
        arrived(plane_in.at[2:32], 1)
        left(line_in.at[0:28], 0)
        left(line_in.at[0:62], 1)

    tgt_out[...] = bias_v[0:2, :] + 0.5 * bias_v[8:10, :] - (0.5 * LN2) * merge(plane_in[...], 2)

    for copy in sends:
        copy.wait_send()


def local(sources, targets, log_src, log_tgt, potential):
    anywhere = pl.BlockSpec(memory_space=pl.ANY)
    vmem = pl.BlockSpec(memory_space=pltpu.VMEM)
    src_out, tgt_out = pl.pallas_call(
        kernel,
        out_shape=[
            jax.ShapeDtypeStruct((ROWS // TILE, TILE), F32),
            jax.ShapeDtypeStruct((BLOCK // TILE, TILE), F32),
        ],
        in_specs=[anywhere] * 5,
        out_specs=[vmem] * 2,
        scratch_shapes=[
            pltpu.VMEM((ROWS, WIDTH), jnp.bfloat16),
            pltpu.VMEM((2 * BLOCK, WIDTH), jnp.bfloat16),
            pltpu.VMEM((PIECES, 4 * PART, WIDTH), jnp.bfloat16),
            pltpu.VMEM((16, TILE), F32),
            pltpu.VMEM((ROWS // TILE, TILE), F32),
            pltpu.VMEM((8, TILE), F32),
            pltpu.VMEM((COLS, TILE), F32),
            pltpu.VMEM((ROWS // TILE, TILE), F32),
            pltpu.VMEM((COLS, ROWS), F32),
            pltpu.VMEM((8 * (2 + PIECES), ROWS), F32),
            pltpu.VMEM((8 * (2 + PIECES), ROWS), F32),
            pltpu.VMEM((8, ROWS), F32),
            pltpu.VMEM((COLS, TILE), F32),
            pltpu.VMEM((COLS, TILE), F32),
            pltpu.VMEM((8, TILE), F32),
            pltpu.VMEM((64, TILE), F32),
            pltpu.VMEM((8, TILE), F32),
            pltpu.VMEM((32, TILE), F32),
            pltpu.SemaphoreType.DMA((8,)),
            pltpu.SemaphoreType.DMA((4 * PIECES + 4,)),
            pltpu.SemaphoreType.DMA((4 * PIECES + 4,)),
            pltpu.SemaphoreType.DMA((4,)),
        ],
        compiler_params=pltpu.CompilerParams(
            collective_id=0, has_side_effects=True, vmem_limit_bytes=56 * 2**20
        ),
        cost_estimate=pl.CostEstimate(
            flops=2 * ROWS * COLS * WIDTH,
            bytes_accessed=2 * WIDTH * (ROWS + COLS),
            transcendentals=2 * ROWS * COLS,
        ),
    )(
        sources,
        targets,
        log_src.reshape(ROWS // TILE, TILE),
        log_tgt.reshape(BLOCK // TILE, TILE),
        potential.reshape(BLOCK // TILE, TILE),
    )
    return src_out.reshape(ROWS), tgt_out.reshape(BLOCK)


def solution(mesh):
    placed = (P(("src", "blk"), None), P("blk", None), P(("src", "blk")), P("blk"), P("blk"))
    return jax.shard_map(
        local, mesh=mesh, in_specs=placed, out_specs=(P(("src", "blk")), P("blk")), check_vma=False
    )
```

```python
import functools
import math

import jax
import jax.numpy as jnp
from jax import lax
from jax.experimental import pallas as pl
from jax.experimental.pallas import tpu as pltpu
from jax.sharding import PartitionSpec as P

MESH = pl.DeviceIdType.MESH
LOG2E = math.log2(math.e)
LN2 = math.log(2.0)
F32 = jnp.float32

ROWS = 2048
COLS = 1024
BLOCK = 256
WIDTH = 1024
TILE = 128
SIDE = 4
PIECES = 2
PART = BLOCK // 2 // PIECES


def dot_t(left, right):
    return lax.dot_general(left, right, (((1,), (1,)), ((), ())), preferred_element_type=F32)


def fold_lanes(op, value):
    while value.shape[1] > TILE:
        half = value.shape[1] // 2
        value = op(value[:, :half], value[:, half:])
    return value


def line_hops(step):
    return min(step, 2 * SIDE - step)


def plane_hops(step):
    return sum(min(n, SIDE - n) for n in divmod(step, SIDE))


def kernel(
    sources,
    targets,
    log_src,
    log_tgt,
    potential,
    src_out,
    tgt_out,
    src_v,
    near_t,
    far_t,
    bias_v,
    weight_v,
    row_bias,
    wide_bias,
    norms,
    scores,
    row_max,
    row_sum,
    shift,
    col_max,
    col_sum,
    col_log,
    line_in,
    line_out,
    plane_in,
    load_sem,
    send_sem,
    recv_sem,
    reduce_sem,
):
    src = lax.axis_index("src")
    blk = lax.axis_index("blk")
    x, y, z_hi = src // (SIDE * SIDE), (src // SIDE) % SIDE, src % SIDE
    z_lo, core = blk // 2, blk % 2
    z = z_hi * 2 + z_lo

    def device(to_x, to_y, to_z, to_core):
        return ((to_x * SIDE + to_y) * SIDE + to_z // 2, (to_z % 2) * 2 + to_core)

    def line(step, to_core):
        return device(x, y, (z + step) % (2 * SIDE), to_core)

    def plane(step, to_core):
        return device((x + step // SIDE) % SIDE, (y + step % SIDE) % SIDE, z, to_core)

    sibling = line(0, 1 - core)
    above, below = line(1, core), line(2 * SIDE - 1, core)

    loads = []

    def load(from_ref, to_ref):
        copy = pltpu.make_async_copy(from_ref, to_ref, load_sem.at[len(loads)])
        copy.start()
        loads.append(copy)
        return copy

    own_rows = pl.ds(pl.multiple_of(core * BLOCK, BLOCK), BLOCK)
    sib_rows = pl.ds(pl.multiple_of((1 - core) * BLOCK, BLOCK), BLOCK)
    load_t = load(targets, near_t.at[own_rows])
    load_p = load(potential, bias_v.at[0:2])
    load_l = load(log_tgt, bias_v.at[8:10])
    load_w = load(log_src, weight_v)
    quarter = ROWS // 4
    load_s = [
        load(sources.at[n * quarter : (n + 1) * quarter], src_v.at[n * quarter : (n + 1) * quarter])
        for n in range(4)
    ]

    barrier = pltpu.get_barrier_semaphore()
    line_steps = sorted(range(1, 2 * SIDE), key=line_hops, reverse=True)
    plane_steps = sorted(range(1, SIDE * SIDE), key=plane_hops, reverse=True)

    def greet(peers):
        for peer in peers:
            pl.semaphore_signal(barrier, inc=1, device_id=peer, device_id_type=MESH)

    lone = [sibling, above, below] + [line(n, 1) for n in line_steps] + [plane(n, 1) for n in plane_steps]
    hub = [sibling] + [line(n, to) for n in line_steps for to in range(2)]
    hub += [plane(n, to) for n in plane_steps for to in range(2)]

    @pl.when(core == 0)
    def _():
        greet(lone)

    @pl.when(core == 1)
    def _():
        greet(hub)

    sends = []

    def send(from_ref, to_ref, number, peer):
        copy = pltpu.make_async_remote_copy(
            src_ref=from_ref,
            dst_ref=to_ref,
            send_sem=send_sem.at[number],
            recv_sem=recv_sem.at[number],
            device_id=peer,
            device_id_type=MESH,
        )
        copy.start()
        sends.append(copy)
        return copy

    core_rows = core * BLOCK
    load_t.wait()
    load_p.wait()
    load_l.wait()
    for half in range(2):
        rows = pl.ds(pl.multiple_of(core_rows + half * TILE, TILE), TILE)
        block = near_t[rows, :].astype(F32)
        tgt_norms = jnp.sum(fold_lanes(jnp.add, block * block).T, axis=0, keepdims=True)
        bias = bias_v[8 + half : 9 + half, :] + 2.0 * bias_v[half : half + 1, :]
        row_bias[pl.ds(core * 2 + half, 1), :] = (bias - tgt_norms / 16.0) * LOG2E

    def widen(slot):
        for half in range(2):
            row = jnp.broadcast_to(row_bias[pl.ds(slot * 2 + half, 1), :], (TILE, TILE))
            wide_bias[pl.ds(pl.multiple_of(slot * BLOCK + half * TILE, TILE), TILE), :] = row.T

    widen(core)
    load_w.wait()
    weights = jnp.concatenate([weight_v[n : n + 1, :] for n in range(ROWS // TILE)], axis=1)
    shift[...] = jnp.broadcast_to(weights * LOG2E, (8, ROWS))

    @pl.when(core == 0)
    def _():
        pl.semaphore_wait(barrier, len(lone))

    @pl.when(core == 1)
    def _():
        pl.semaphore_wait(barrier, len(hub))

    up, down = [], []
    own_bias = row_bias.at[pl.ds(core * 2, 2)]
    far_bias = row_bias.at[pl.ds(4 + core * 2, 2)]
    bias_far = send(own_bias, far_bias, 4 * PIECES + 2, above)
    for piece in range(PIECES):
        low = pl.ds(pl.multiple_of(core_rows + piece * PART, PART), PART)
        high = pl.ds(pl.multiple_of(core_rows + BLOCK // 2 + piece * PART, PART), PART)
        land_low = pl.ds(pl.multiple_of(core * 2 * PART, PART), PART)
        land_high = pl.ds(pl.multiple_of(core * 2 * PART + PART, PART), PART)
        up.append(send(near_t.at[low], far_t.at[piece, land_low], 4 * piece, above))
        down.append(send(near_t.at[high], far_t.at[piece, land_high], 4 * piece + 1, below))
    near = send(near_t.at[own_rows], near_t.at[own_rows], 4 * PIECES, sibling)
    own_bias = row_bias.at[pl.ds(core * 2, 2)]
    far_bias = row_bias.at[pl.ds(4 + core * 2, 2)]
    bias_near = send(own_bias, own_bias, 4 * PIECES + 1, sibling)

    def row_pass(moving, segments, parts, waits=()):
        length = moving.shape[0] // len(segments)
        for part in parts:
            if waits:
                waits[part].wait()
            bias = [wide_bias[rows, :] for rows in segments]
            bias = bias[0] if len(bias) == 1 else jnp.concatenate(bias, axis=0)
            inner = dot_t(moving[...], src_v[part * quarter : (part + 1) * quarter, :])
            for tile in range(quarter // TILE):
                lanes = pl.ds(part * quarter + tile * TILE, TILE)
                value = inner[:, tile * TILE : (tile + 1) * TILE] * (LOG2E / 8.0) + bias
                for at, rows in enumerate(segments):
                    scores[rows, lanes] = value[at * length : (at + 1) * length, :]
                deep = value.reshape(-1, 8, TILE)
                top = jnp.max(deep, axis=0)
                if waits:
                    row_sum[:, lanes] = jnp.sum(jnp.exp2(deep - top[None]), axis=0)
                else:
                    before = row_max[:, lanes]
                    top = jnp.maximum(top, before)
                    row_sum[:, lanes] = row_sum[:, lanes] * jnp.exp2(before - top) + jnp.sum(
                        jnp.exp2(deep - top[None]), axis=0
                    )
                row_max[:, lanes] = top

    row_pass(near_t.at[own_rows], [own_rows], range(4), load_s)
    near.wait_recv()
    bias_near.wait_recv()
    widen(1 - core)
    row_pass(near_t.at[sib_rows], [sib_rows], range(4))

    for tile in range(ROWS // TILE):
        block = src_v[tile * TILE : (tile + 1) * TILE, :].astype(F32)
        norms[tile : tile + 1, :] = jnp.sum(fold_lanes(jnp.add, block * block).T, axis=0, keepdims=True)
    bias_far.wait_recv()
    bias_pass = send(far_bias, far_bias, 4 * PIECES + 3, sibling)

    def pass_on(piece):
        up[piece].wait_recv()
        down[piece].wait_recv()
        land = far_t.at[piece, pl.ds(pl.multiple_of(core * 2 * PART, 2 * PART), 2 * PART)]
        return send(land, land, 4 * piece + 2, sibling)

    passed = pass_on(0)
    bias_pass.wait_recv()
    widen(2)
    widen(3)
    for piece in range(PIECES):
        segments = [
            pl.ds(2 * BLOCK + of_core * BLOCK + half * (BLOCK // 2) + piece * PART, PART)
            for of_core in range(2)
            for half in range(2)
        ]
        passed.wait_recv()
        if piece + 1 < PIECES:
            row_pass(far_t.at[piece], segments, range(2))
            passed = pass_on(piece + 1)
            row_pass(far_t.at[piece], segments, range(2, 4))
        else:
            row_pass(far_t.at[piece], segments, range(4))

    peak, total = row_max[...], row_sum[...]
    top = jnp.max(peak, axis=0, keepdims=True)
    row_log = top + jnp.log2(jnp.sum(total * jnp.exp2(peak - top), axis=0, keepdims=True))
    shift[...] = shift[...] - row_log
    row_max[0:1, :] = row_log

    for block in range(COLS // TILE):
        for group in range(TILE // 8):
            rows = pl.ds(block * TILE + group * 8, 8)
            value = scores[rows, :] + shift[...]
            peak = fold_lanes(jnp.maximum, value)
            deep = jnp.concatenate([peak] * (ROWS // TILE), axis=1)
            col_max[rows, :] = peak
            col_sum[rows, :] = fold_lanes(jnp.add, jnp.exp2(value - deep))
        rows = pl.ds(block * TILE, TILE)
        peaks = col_max[rows, :].T
        peak = jnp.max(peaks, axis=0, keepdims=True)
        total = jnp.sum(col_sum[rows, :].T * jnp.exp2(peaks - peak), axis=0, keepdims=True)
        col_log[block : block + 1, :] = peak + jnp.log2(total)

    def reduce_send(from_ref, to_ref, stage, peer):
        copy = pltpu.make_async_remote_copy(
            src_ref=from_ref,
            dst_ref=to_ref,
            send_sem=reduce_sem.at[2 * stage],
            recv_sem=reduce_sem.at[2 * stage + 1],
            device_id=peer,
            device_id_type=MESH,
        )
        copy.start()
        return copy

    def arrived(ref, stage):
        pltpu.make_async_copy(ref, ref, reduce_sem.at[2 * stage + 1]).wait()

    def left(ref, stage):
        pltpu.make_async_copy(ref, ref, reduce_sem.at[2 * stage]).wait()

    def merge(value, rows):
        deep = value.reshape(-1, 8, TILE)
        peak = jnp.max(deep, axis=0)
        total = jnp.sum(jnp.exp2(deep - peak[None]), axis=0)
        parts = [slice(n, n + rows) for n in range(0, 8, rows)]
        top = functools.reduce(jnp.maximum, [peak[p] for p in parts])
        return top + jnp.log2(sum(total[p] * jnp.exp2(peak[p] - top) for p in parts))

    for step in line_steps:
        part = col_log.at[4 * (step % 2) : 4 * (step % 2) + 4]
        slot = pl.ds(pl.multiple_of(8 * step + 4 * core, 4), 4)
        reduce_send(part, line_in.at[slot], 0, line(step, 1))

    for tile in range(ROWS // TILE):
        lanes = pl.ds(tile * TILE, TILE)
        src_out[lanes] = (
            norms[tile : tile + 1, :] / 32.0 - 64.0 - (0.5 * LN2) * row_max[0:1, lanes]
        ).reshape(TILE)

    @pl.when(core == 0)
    def _():
        reduce_send(col_log.at[0:4], line_in.at[0:4], 0, sibling)
        arrived(plane_in, 1)
        left(line_in.at[0:32], 0)

    @pl.when(core == 1)
    def _():
        line_in[4:8, :] = col_log[0:4, :]
        arrived(line_in.at[0:60], 0)
        line_out[0:4, :] = merge(line_in[...], 4)
        for step in plane_steps:
            for to in range(2):
                reduce_send(
                    line_out.at[2 * to : 2 * to + 2], plane_in.at[2 * step : 2 * step + 2], 1, plane(step, to)
                )
        reduce_send(line_out.at[0:2], plane_in.at[0:2], 1, sibling)
        plane_in[0:2, :] = line_out[2:4, :]
        arrived(plane_in.at[2:32], 1)
        left(line_in.at[0:28], 0)
        left(line_in.at[0:62], 1)

    tgt_new = bias_v[0:2, :] + 0.5 * bias_v[8:10, :] - (0.5 * LN2) * merge(plane_in[...], 2)
    for half in range(2):
        tgt_out[half * TILE : (half + 1) * TILE] = tgt_new[half : half + 1, :].reshape(TILE)

    for copy in sends:
        copy.wait_send()


def finish(src_in, tgt_in, src_out, tgt_out, sem):
    one = pltpu.make_async_copy(src_in, src_out, sem.at[0])
    two = pltpu.make_async_copy(tgt_in, tgt_out, sem.at[1])
    one.start()
    two.start()
    one.wait()
    two.wait()


def local(sources, targets, log_src, log_tgt, potential):
    anywhere = pl.BlockSpec(memory_space=pl.ANY)
    vmem = pl.BlockSpec(memory_space=pltpu.VMEM)
    src_out, tgt_out = pl.pallas_call(
        kernel,
        out_shape=[
            pltpu.VMEM((ROWS,), F32),
            pltpu.VMEM((BLOCK,), F32),
        ],
        in_specs=[anywhere] * 5,
        out_specs=[vmem] * 2,
        scratch_shapes=[
            pltpu.VMEM((ROWS, WIDTH), jnp.bfloat16),
            pltpu.VMEM((2 * BLOCK, WIDTH), jnp.bfloat16),
            pltpu.VMEM((PIECES, 4 * PART, WIDTH), jnp.bfloat16),
            pltpu.VMEM((16, TILE), F32),
            pltpu.VMEM((ROWS // TILE, TILE), F32),
            pltpu.VMEM((8, TILE), F32),
            pltpu.VMEM((COLS, TILE), F32),
            pltpu.VMEM((ROWS // TILE, TILE), F32),
            pltpu.VMEM((COLS, ROWS), F32),
            pltpu.VMEM((8, ROWS), F32),
            pltpu.VMEM((8, ROWS), F32),
            pltpu.VMEM((8, ROWS), F32),
            pltpu.VMEM((COLS, TILE), F32),
            pltpu.VMEM((COLS, TILE), F32),
            pltpu.VMEM((8, TILE), F32),
            pltpu.VMEM((64, TILE), F32),
            pltpu.VMEM((8, TILE), F32),
            pltpu.VMEM((32, TILE), F32),
            pltpu.SemaphoreType.DMA((8,)),
            pltpu.SemaphoreType.DMA((4 * PIECES + 4,)),
            pltpu.SemaphoreType.DMA((4 * PIECES + 4,)),
            pltpu.SemaphoreType.DMA((4,)),
        ],
        compiler_params=pltpu.CompilerParams(
            collective_id=0, has_side_effects=True, vmem_limit_bytes=56 * 2**20
        ),
        cost_estimate=pl.CostEstimate(
            flops=2 * ROWS * COLS * WIDTH,
            bytes_accessed=2 * WIDTH * (ROWS + COLS),
            transcendentals=2 * ROWS * COLS,
        ),
    )(
        sources,
        targets,
        log_src.reshape(ROWS // TILE, TILE),
        log_tgt.reshape(BLOCK // TILE, TILE),
        potential.reshape(BLOCK // TILE, TILE),
    )
    return pl.pallas_call(
        finish,
        out_shape=[jax.ShapeDtypeStruct((ROWS,), F32), jax.ShapeDtypeStruct((BLOCK,), F32)],
        in_specs=[vmem] * 2,
        out_specs=[anywhere] * 2,
        scratch_shapes=[pltpu.SemaphoreType.DMA((2,))],
    )(
        pltpu.with_memory_space_constraint(src_out, pltpu.VMEM),
        pltpu.with_memory_space_constraint(tgt_out, pltpu.VMEM),
    )


def solution(mesh):
    placed = (P(("src", "blk"), None), P("blk", None), P(("src", "blk")), P("blk"), P("blk"))
    return jax.shard_map(
        local, mesh=mesh, in_specs=placed, out_specs=(P(("src", "blk")), P("blk")), check_vma=False
    )
```

```python
import functools
import math

import jax
import jax.numpy as jnp
from jax import lax
from jax.experimental import pallas as pl
from jax.experimental.pallas import tpu as pltpu
from jax.sharding import PartitionSpec as P

MESH = pl.DeviceIdType.MESH
LOG2E = math.log2(math.e)
LN2 = math.log(2.0)
F32 = jnp.float32

ROWS = 2048
COLS = 1024
BLOCK = 256
WIDTH = 1024
TILE = 128
SIDE = 4
PIECES = 2
PART = BLOCK // 2 // PIECES


def dot_t(left, right):
    return lax.dot_general(left, right, (((1,), (1,)), ((), ())), preferred_element_type=F32)


def fold_lanes(op, value):
    while value.shape[1] > TILE:
        half = value.shape[1] // 2
        value = op(value[:, :half], value[:, half:])
    return value


def line_hops(step):
    return min(step, 2 * SIDE - step)


def plane_hops(step):
    return sum(min(n, SIDE - n) for n in divmod(step, SIDE))


def kernel(
    sources,
    targets,
    log_src,
    log_tgt,
    potential,
    src_out,
    tgt_out,
    src_v,
    near_t,
    far_t,
    bias_v,
    weight_v,
    row_bias,
    wide_bias,
    norms,
    scores,
    row_max,
    row_sum,
    shift,
    col_max,
    col_sum,
    col_log,
    line_in,
    line_out,
    plane_in,
    load_sem,
    send_sem,
    recv_sem,
    reduce_sem,
    news_sem,
):
    src = lax.axis_index("src")
    blk = lax.axis_index("blk")
    x, y, z_hi = src // (SIDE * SIDE), (src // SIDE) % SIDE, src % SIDE
    z_lo, core = blk // 2, blk % 2
    z = z_hi * 2 + z_lo

    def device(to_x, to_y, to_z, to_core):
        return ((to_x * SIDE + to_y) * SIDE + to_z // 2, (to_z % 2) * 2 + to_core)

    def line(step, to_core):
        return device(x, y, (z + step) % (2 * SIDE), to_core)

    def plane(step, to_core):
        return device((x + step // SIDE) % SIDE, (y + step % SIDE) % SIDE, z, to_core)

    sibling = line(0, 1 - core)
    above, below = line(1, core), line(2 * SIDE - 1, core)

    loads = []

    def load(from_ref, to_ref):
        copy = pltpu.make_async_copy(from_ref, to_ref, load_sem.at[len(loads)])
        copy.start()
        loads.append(copy)
        return copy

    own_rows = pl.ds(pl.multiple_of(core * BLOCK, BLOCK), BLOCK)
    sib_rows = pl.ds(pl.multiple_of((1 - core) * BLOCK, BLOCK), BLOCK)
    load_t = load(targets, near_t.at[own_rows])
    load_p = load(potential, bias_v.at[0:2])
    load_l = load(log_tgt, bias_v.at[8:10])
    load_w = load(log_src, weight_v)
    quarter = ROWS // 4
    load_s = [
        load(sources.at[n * quarter : (n + 1) * quarter], src_v.at[n * quarter : (n + 1) * quarter])
        for n in range(4)
    ]

    barrier = pltpu.get_barrier_semaphore()
    line_steps = sorted(range(1, 2 * SIDE), key=line_hops, reverse=True)
    plane_steps = sorted(range(1, SIDE * SIDE), key=plane_hops, reverse=True)

    def greet(peers):
        for peer in peers:
            pl.semaphore_signal(barrier, inc=1, device_id=peer, device_id_type=MESH)

    x_sides = [plane(n * SIDE, 1) for n in (1, SIDE - 1)]
    y_sides = [plane(n, 1) for n in (1, SIDE - 1)]
    lone = [sibling, above, below]
    hub = lone + x_sides + y_sides

    @pl.when(core == 0)
    def _():
        greet(lone)

    @pl.when(core == 1)
    def _():
        greet(hub)

    sends = []

    def send(from_ref, to_ref, number, peer):
        copy = pltpu.make_async_remote_copy(
            src_ref=from_ref,
            dst_ref=to_ref,
            send_sem=send_sem.at[number],
            recv_sem=recv_sem.at[number],
            device_id=peer,
            device_id_type=MESH,
        )
        copy.start()
        sends.append(copy)
        return copy

    core_rows = core * BLOCK
    load_t.wait()
    load_p.wait()
    load_l.wait()
    for half in range(2):
        rows = pl.ds(pl.multiple_of(core_rows + half * TILE, TILE), TILE)
        block = near_t[rows, :].astype(F32)
        tgt_norms = jnp.sum(fold_lanes(jnp.add, block * block).T, axis=0, keepdims=True)
        bias = bias_v[8 + half : 9 + half, :] + 2.0 * bias_v[half : half + 1, :]
        row_bias[pl.ds(core * 2 + half, 1), :] = (bias - tgt_norms / 16.0) * LOG2E

    def widen(slot):
        for half in range(2):
            row = jnp.broadcast_to(row_bias[pl.ds(slot * 2 + half, 1), :], (TILE, TILE))
            wide_bias[pl.ds(pl.multiple_of(slot * BLOCK + half * TILE, TILE), TILE), :] = row.T

    widen(core)
    load_w.wait()
    weights = jnp.concatenate([weight_v[n : n + 1, :] for n in range(ROWS // TILE)], axis=1)
    shift[...] = jnp.broadcast_to(weights * LOG2E, (8, ROWS))

    @pl.when(core == 0)
    def _():
        pl.semaphore_wait(barrier, len(lone))

    @pl.when(core == 1)
    def _():
        pl.semaphore_wait(barrier, len(hub))

    up, down = [], []
    own_bias = row_bias.at[pl.ds(core * 2, 2)]
    far_bias = row_bias.at[pl.ds(4 + core * 2, 2)]
    bias_far = send(own_bias, far_bias, 4 * PIECES + 2, above)
    for piece in range(PIECES):
        low = pl.ds(pl.multiple_of(core_rows + piece * PART, PART), PART)
        high = pl.ds(pl.multiple_of(core_rows + BLOCK // 2 + piece * PART, PART), PART)
        land_low = pl.ds(pl.multiple_of(core * 2 * PART, PART), PART)
        land_high = pl.ds(pl.multiple_of(core * 2 * PART + PART, PART), PART)
        up.append(send(near_t.at[low], far_t.at[piece, land_low], 4 * piece, above))
        down.append(send(near_t.at[high], far_t.at[piece, land_high], 4 * piece + 1, below))
    near = send(near_t.at[own_rows], near_t.at[own_rows], 4 * PIECES, sibling)
    own_bias = row_bias.at[pl.ds(core * 2, 2)]
    far_bias = row_bias.at[pl.ds(4 + core * 2, 2)]
    bias_near = send(own_bias, own_bias, 4 * PIECES + 1, sibling)

    def news(number, amount):
        pl.semaphore_wait(news_sem.at[number], amount)

    def tell(number, peers):
        for peer in peers:
            pl.semaphore_signal(news_sem.at[number], inc=1, device_id=peer, device_id_type=MESH)

    @pl.when(core == 1)
    def _():
        tell(0, [above, below])
        tell(1, x_sides)

    def row_pass(moving, segments, parts, waits=()):
        length = moving.shape[0] // len(segments)
        for part in parts:
            if waits:
                waits[part].wait()
            bias = [wide_bias[rows, :] for rows in segments]
            bias = bias[0] if len(bias) == 1 else jnp.concatenate(bias, axis=0)
            inner = dot_t(moving[...], src_v[part * quarter : (part + 1) * quarter, :])
            for tile in range(quarter // TILE):
                lanes = pl.ds(part * quarter + tile * TILE, TILE)
                value = inner[:, tile * TILE : (tile + 1) * TILE] * (LOG2E / 8.0) + bias
                for at, rows in enumerate(segments):
                    scores[rows, lanes] = value[at * length : (at + 1) * length, :]
                deep = value.reshape(-1, 8, TILE)
                top = jnp.max(deep, axis=0)
                if waits:
                    row_sum[:, lanes] = jnp.sum(jnp.exp2(deep - top[None]), axis=0)
                else:
                    before = row_max[:, lanes]
                    top = jnp.maximum(top, before)
                    row_sum[:, lanes] = row_sum[:, lanes] * jnp.exp2(before - top) + jnp.sum(
                        jnp.exp2(deep - top[None]), axis=0
                    )
                row_max[:, lanes] = top

    row_pass(near_t.at[own_rows], [own_rows], range(4), load_s)
    near.wait_recv()
    bias_near.wait_recv()
    widen(1 - core)
    row_pass(near_t.at[sib_rows], [sib_rows], range(4))

    @pl.when(core == 1)
    def _():
        news(0, 2)
        news(1, 2)
        tell(2, [line(2, 1), line(2 * SIDE - 2, 1)])
        tell(3, [plane(2 * SIDE, 1)])

    for tile in range(ROWS // TILE):
        block = src_v[tile * TILE : (tile + 1) * TILE, :].astype(F32)
        norms[tile : tile + 1, :] = jnp.sum(fold_lanes(jnp.add, block * block).T, axis=0, keepdims=True)
    bias_far.wait_recv()
    bias_pass = send(far_bias, far_bias, 4 * PIECES + 3, sibling)

    def pass_on(piece):
        up[piece].wait_recv()
        down[piece].wait_recv()
        land = far_t.at[piece, pl.ds(pl.multiple_of(core * 2 * PART, 2 * PART), 2 * PART)]
        return send(land, land, 4 * piece + 2, sibling)

    passed = pass_on(0)

    @pl.when(core == 1)
    def _():
        news(2, 2)
        news(3, 1)
        tell(4, [sibling])
        tell(5, y_sides)

    bias_pass.wait_recv()
    widen(2)
    widen(3)
    for piece in range(PIECES):
        segments = [
            pl.ds(2 * BLOCK + of_core * BLOCK + half * (BLOCK // 2) + piece * PART, PART)
            for of_core in range(2)
            for half in range(2)
        ]
        passed.wait_recv()
        if piece + 1 < PIECES:
            row_pass(far_t.at[piece], segments, range(2))
            passed = pass_on(piece + 1)

            @pl.when(core == 1)
            def _():
                news(5, 2)
                tell(6, [plane(SIDE // 2, 1)])

            row_pass(far_t.at[piece], segments, range(2, 4))
        else:
            row_pass(far_t.at[piece], segments, range(4))

    peak, total = row_max[...], row_sum[...]
    top = jnp.max(peak, axis=0, keepdims=True)
    row_log = top + jnp.log2(jnp.sum(total * jnp.exp2(peak - top), axis=0, keepdims=True))
    shift[...] = shift[...] - row_log
    row_max[0:1, :] = row_log

    for block in range(COLS // TILE):
        for group in range(TILE // 8):
            rows = pl.ds(block * TILE + group * 8, 8)
            value = scores[rows, :] + shift[...]
            peak = fold_lanes(jnp.maximum, value)
            deep = jnp.concatenate([peak] * (ROWS // TILE), axis=1)
            col_max[rows, :] = peak
            col_sum[rows, :] = fold_lanes(jnp.add, jnp.exp2(value - deep))
        rows = pl.ds(block * TILE, TILE)
        peaks = col_max[rows, :].T
        peak = jnp.max(peaks, axis=0, keepdims=True)
        total = jnp.sum(col_sum[rows, :].T * jnp.exp2(peaks - peak), axis=0, keepdims=True)
        col_log[block : block + 1, :] = peak + jnp.log2(total)

    def reduce_send(from_ref, to_ref, stage, peer):
        copy = pltpu.make_async_remote_copy(
            src_ref=from_ref,
            dst_ref=to_ref,
            send_sem=reduce_sem.at[2 * stage],
            recv_sem=reduce_sem.at[2 * stage + 1],
            device_id=peer,
            device_id_type=MESH,
        )
        copy.start()
        return copy

    def arrived(ref, stage):
        pltpu.make_async_copy(ref, ref, reduce_sem.at[2 * stage + 1]).wait()

    def left(ref, stage):
        pltpu.make_async_copy(ref, ref, reduce_sem.at[2 * stage]).wait()

    def merge(value, rows):
        deep = value.reshape(-1, 8, TILE)
        peak = jnp.max(deep, axis=0)
        total = jnp.sum(jnp.exp2(deep - peak[None]), axis=0)
        parts = [slice(n, n + rows) for n in range(0, 8, rows)]
        top = functools.reduce(jnp.maximum, [peak[p] for p in parts])
        return top + jnp.log2(sum(total[p] * jnp.exp2(peak[p] - top) for p in parts))

    @pl.when(core == 0)
    def _():
        news(4, 1)

    for step in line_steps:
        part = col_log.at[4 * (step % 2) : 4 * (step % 2) + 4]
        slot = pl.ds(pl.multiple_of(8 * step + 4 * core, 4), 4)
        reduce_send(part, line_in.at[slot], 0, line(step, 1))

    for tile in range(ROWS // TILE):
        lanes = pl.ds(tile * TILE, TILE)
        src_out[lanes] = (
            norms[tile : tile + 1, :] / 32.0 - 64.0 - (0.5 * LN2) * row_max[0:1, lanes]
        ).reshape(TILE)

    @pl.when(core == 0)
    def _():
        reduce_send(col_log.at[0:4], line_in.at[0:4], 0, sibling)
        arrived(plane_in, 1)
        left(line_in.at[0:32], 0)

    @pl.when(core == 1)
    def _():
        line_in[4:8, :] = col_log[0:4, :]
        arrived(line_in.at[0:60], 0)
        line_out[0:4, :] = merge(line_in[...], 4)
        news(6, 1)
        for step in plane_steps:
            for to in range(2):
                reduce_send(
                    line_out.at[2 * to : 2 * to + 2], plane_in.at[2 * step : 2 * step + 2], 1, plane(step, to)
                )
        reduce_send(line_out.at[0:2], plane_in.at[0:2], 1, sibling)
        plane_in[0:2, :] = line_out[2:4, :]
        arrived(plane_in.at[2:32], 1)
        left(line_in.at[0:28], 0)
        left(line_in.at[0:62], 1)

    tgt_new = bias_v[0:2, :] + 0.5 * bias_v[8:10, :] - (0.5 * LN2) * merge(plane_in[...], 2)
    for half in range(2):
        tgt_out[half * TILE : (half + 1) * TILE] = tgt_new[half : half + 1, :].reshape(TILE)

    for copy in sends:
        copy.wait_send()


def finish(src_in, tgt_in, src_out, tgt_out, sem):
    one = pltpu.make_async_copy(src_in, src_out, sem.at[0])
    two = pltpu.make_async_copy(tgt_in, tgt_out, sem.at[1])
    one.start()
    two.start()
    one.wait()
    two.wait()


def local(sources, targets, log_src, log_tgt, potential):
    anywhere = pl.BlockSpec(memory_space=pl.ANY)
    vmem = pl.BlockSpec(memory_space=pltpu.VMEM)
    src_out, tgt_out = pl.pallas_call(
        kernel,
        out_shape=[
            pltpu.VMEM((ROWS,), F32),
            pltpu.VMEM((BLOCK,), F32),
        ],
        in_specs=[anywhere] * 5,
        out_specs=[vmem] * 2,
        scratch_shapes=[
            pltpu.VMEM((ROWS, WIDTH), jnp.bfloat16),
            pltpu.VMEM((2 * BLOCK, WIDTH), jnp.bfloat16),
            pltpu.VMEM((PIECES, 4 * PART, WIDTH), jnp.bfloat16),
            pltpu.VMEM((16, TILE), F32),
            pltpu.VMEM((ROWS // TILE, TILE), F32),
            pltpu.VMEM((8, TILE), F32),
            pltpu.VMEM((COLS, TILE), F32),
            pltpu.VMEM((ROWS // TILE, TILE), F32),
            pltpu.VMEM((COLS, ROWS), F32),
            pltpu.VMEM((8, ROWS), F32),
            pltpu.VMEM((8, ROWS), F32),
            pltpu.VMEM((8, ROWS), F32),
            pltpu.VMEM((COLS, TILE), F32),
            pltpu.VMEM((COLS, TILE), F32),
            pltpu.VMEM((8, TILE), F32),
            pltpu.VMEM((64, TILE), F32),
            pltpu.VMEM((8, TILE), F32),
            pltpu.VMEM((32, TILE), F32),
            pltpu.SemaphoreType.DMA((8,)),
            pltpu.SemaphoreType.DMA((4 * PIECES + 4,)),
            pltpu.SemaphoreType.DMA((4 * PIECES + 4,)),
            pltpu.SemaphoreType.DMA((4,)),
            pltpu.SemaphoreType.REGULAR((7,)),
        ],
        compiler_params=pltpu.CompilerParams(
            collective_id=0, has_side_effects=True, vmem_limit_bytes=56 * 2**20
        ),
        cost_estimate=pl.CostEstimate(
            flops=2 * ROWS * COLS * WIDTH,
            bytes_accessed=2 * WIDTH * (ROWS + COLS),
            transcendentals=2 * ROWS * COLS,
        ),
    )(
        sources,
        targets,
        log_src.reshape(ROWS // TILE, TILE),
        log_tgt.reshape(BLOCK // TILE, TILE),
        potential.reshape(BLOCK // TILE, TILE),
    )
    return pl.pallas_call(
        finish,
        out_shape=[jax.ShapeDtypeStruct((ROWS,), F32), jax.ShapeDtypeStruct((BLOCK,), F32)],
        in_specs=[vmem] * 2,
        out_specs=[anywhere] * 2,
        scratch_shapes=[pltpu.SemaphoreType.DMA((2,))],
    )(
        pltpu.with_memory_space_constraint(src_out, pltpu.VMEM),
        pltpu.with_memory_space_constraint(tgt_out, pltpu.VMEM),
    )


def solution(mesh):
    placed = (P(("src", "blk"), None), P("blk", None), P(("src", "blk")), P("blk"), P("blk"))
    return jax.shard_map(
        local, mesh=mesh, in_specs=placed, out_specs=(P(("src", "blk")), P("blk")), check_vma=False
    )
```

```python
import functools
import math

import jax
import jax.numpy as jnp
from jax import lax
from jax.experimental import pallas as pl
from jax.experimental.pallas import tpu as pltpu
from jax.sharding import PartitionSpec as P

MESH = pl.DeviceIdType.MESH
LOG2E = math.log2(math.e)
LN2 = math.log(2.0)
F32 = jnp.float32

ROWS = 2048
COLS = 1024
BLOCK = 256
WIDTH = 1024
TILE = 128
SIDE = 4
PIECES = 2
PART = BLOCK // 2 // PIECES


def dot_t(left, right):
    return lax.dot_general(left, right, (((1,), (1,)), ((), ())), preferred_element_type=F32)


def fold_lanes(op, value):
    while value.shape[1] > TILE:
        half = value.shape[1] // 2
        value = op(value[:, :half], value[:, half:])
    return value


def line_hops(step):
    return min(step, 2 * SIDE - step)


def plane_hops(step):
    return sum(min(n, SIDE - n) for n in divmod(step, SIDE))


def kernel(
    sources,
    targets,
    log_src,
    log_tgt,
    potential,
    src_out,
    tgt_out,
    src_v,
    near_t,
    far_t,
    bias_v,
    weight_v,
    row_bias,
    wide_bias,
    norms,
    scores,
    row_max,
    row_sum,
    shift,
    col_max,
    col_sum,
    col_log,
    line_in,
    line_out,
    plane_in,
    load_sem,
    send_sem,
    recv_sem,
    reduce_sem,
    news_sem,
):
    src = lax.axis_index("src")
    blk = lax.axis_index("blk")
    x, y, z_hi = src // (SIDE * SIDE), (src // SIDE) % SIDE, src % SIDE
    z_lo, core = blk // 2, blk % 2
    z = z_hi * 2 + z_lo

    def device(to_x, to_y, to_z, to_core):
        return ((to_x * SIDE + to_y) * SIDE + to_z // 2, (to_z % 2) * 2 + to_core)

    def line(step, to_core):
        return device(x, y, (z + step) % (2 * SIDE), to_core)

    def plane(step, to_core):
        return device((x + step // SIDE) % SIDE, (y + step % SIDE) % SIDE, z, to_core)

    sibling = line(0, 1 - core)
    above, below = line(1, core), line(2 * SIDE - 1, core)

    loads = []

    def load(from_ref, to_ref):
        copy = pltpu.make_async_copy(from_ref, to_ref, load_sem.at[len(loads)])
        copy.start()
        loads.append(copy)
        return copy

    own_rows = pl.ds(pl.multiple_of(core * BLOCK, BLOCK), BLOCK)
    sib_rows = pl.ds(pl.multiple_of((1 - core) * BLOCK, BLOCK), BLOCK)
    load_t = load(targets, near_t.at[own_rows])
    load_p = load(potential, bias_v.at[0:2])
    load_l = load(log_tgt, bias_v.at[8:10])
    load_w = load(log_src, weight_v)
    quarter = ROWS // 4
    load_s = [
        load(sources.at[n * quarter : (n + 1) * quarter], src_v.at[n * quarter : (n + 1) * quarter])
        for n in range(4)
    ]

    barrier = pltpu.get_barrier_semaphore()
    line_steps = sorted(range(1, 2 * SIDE), key=line_hops, reverse=True)
    plane_steps = sorted(range(1, SIDE * SIDE), key=plane_hops, reverse=True)

    def greet(peers):
        for peer in peers:
            pl.semaphore_signal(barrier, inc=1, device_id=peer, device_id_type=MESH)

    x_sides = [plane(n * SIDE, 1) for n in (1, SIDE - 1)]
    y_sides = [plane(n, 1) for n in (1, SIDE - 1)]
    lone = [sibling, above, below]
    hub = lone + x_sides + y_sides

    @pl.when(core == 0)
    def _():
        greet(lone)

    @pl.when(core == 1)
    def _():
        greet(hub)

    sends = []

    def send(from_ref, to_ref, number, peer):
        copy = pltpu.make_async_remote_copy(
            src_ref=from_ref,
            dst_ref=to_ref,
            send_sem=send_sem.at[number],
            recv_sem=recv_sem.at[number],
            device_id=peer,
            device_id_type=MESH,
        )
        copy.start()
        sends.append(copy)
        return copy

    core_rows = core * BLOCK
    load_t.wait()
    load_p.wait()
    load_l.wait()
    for half in range(2):
        rows = pl.ds(pl.multiple_of(core_rows + half * TILE, TILE), TILE)
        block = near_t[rows, :].astype(F32)
        tgt_norms = jnp.sum(fold_lanes(jnp.add, block * block).T, axis=0, keepdims=True)
        bias = bias_v[8 + half : 9 + half, :] + 2.0 * bias_v[half : half + 1, :]
        row_bias[pl.ds(core * 2 + half, 1), :] = (bias - tgt_norms / 16.0) * LOG2E

    def widen(slot):
        for half in range(2):
            row = jnp.broadcast_to(row_bias[pl.ds(slot * 2 + half, 1), :], (TILE, TILE))
            wide_bias[pl.ds(pl.multiple_of(slot * BLOCK + half * TILE, TILE), TILE), :] = row.T

    widen(core)
    load_w.wait()
    weights = jnp.concatenate([weight_v[n : n + 1, :] for n in range(ROWS // TILE)], axis=1)
    shift[...] = jnp.broadcast_to(weights * LOG2E, (8, ROWS))

    @pl.when(core == 0)
    def _():
        pl.semaphore_wait(barrier, len(lone))

    @pl.when(core == 1)
    def _():
        pl.semaphore_wait(barrier, len(hub))

    up, down = [], []
    own_bias = row_bias.at[pl.ds(core * 2, 2)]
    far_bias = row_bias.at[pl.ds(4 + core * 2, 2)]
    bias_far = send(own_bias, far_bias, 4 * PIECES + 2, above)
    for piece in range(PIECES):
        low = pl.ds(pl.multiple_of(core_rows + piece * PART, PART), PART)
        high = pl.ds(pl.multiple_of(core_rows + BLOCK // 2 + piece * PART, PART), PART)
        land_low = pl.ds(pl.multiple_of(core * 2 * PART, PART), PART)
        land_high = pl.ds(pl.multiple_of(core * 2 * PART + PART, PART), PART)
        up.append(send(near_t.at[low], far_t.at[piece, land_low], 4 * piece, above))
        down.append(send(near_t.at[high], far_t.at[piece, land_high], 4 * piece + 1, below))
    near = send(near_t.at[own_rows], near_t.at[own_rows], 4 * PIECES, sibling)
    own_bias = row_bias.at[pl.ds(core * 2, 2)]
    far_bias = row_bias.at[pl.ds(4 + core * 2, 2)]
    bias_near = send(own_bias, own_bias, 4 * PIECES + 1, sibling)

    def news(number, amount):
        pl.semaphore_wait(news_sem.at[number], amount)

    def tell(number, peers):
        for peer in peers:
            pl.semaphore_signal(news_sem.at[number], inc=1, device_id=peer, device_id_type=MESH)

    @pl.when(core == 1)
    def _():
        tell(0, [above, below])
        tell(1, x_sides)

    def row_pass(moving, segments, parts, waits=()):
        length = moving.shape[0] // len(segments)
        for part in parts:
            if waits:
                waits[part].wait()
            bias = [wide_bias[rows, :] for rows in segments]
            bias = bias[0] if len(bias) == 1 else jnp.concatenate(bias, axis=0)
            inner = dot_t(moving[...], src_v[part * quarter : (part + 1) * quarter, :])
            for tile in range(quarter // TILE):
                lanes = pl.ds(part * quarter + tile * TILE, TILE)
                value = inner[:, tile * TILE : (tile + 1) * TILE] * (LOG2E / 8.0) + bias
                for at, rows in enumerate(segments):
                    scores[rows, lanes] = value[at * length : (at + 1) * length, :]
                deep = value.reshape(-1, 8, TILE)
                top = jnp.max(deep, axis=0)
                if waits:
                    row_sum[:, lanes] = jnp.sum(jnp.exp2(deep - top[None]), axis=0)
                else:
                    before = row_max[:, lanes]
                    top = jnp.maximum(top, before)
                    row_sum[:, lanes] = row_sum[:, lanes] * jnp.exp2(before - top) + jnp.sum(
                        jnp.exp2(deep - top[None]), axis=0
                    )
                row_max[:, lanes] = top

    row_pass(near_t.at[own_rows], [own_rows], range(4), load_s)
    near.wait_recv()
    bias_near.wait_recv()
    widen(1 - core)
    row_pass(near_t.at[sib_rows], [sib_rows], range(4))

    @pl.when(core == 1)
    def _():
        news(0, 2)
        news(1, 2)
        tell(2, [line(2, 1), line(2 * SIDE - 2, 1)])
        tell(3, [plane(2 * SIDE, 1)])

    for tile in range(ROWS // TILE):
        block = src_v[tile * TILE : (tile + 1) * TILE, :].astype(F32)
        norms[tile : tile + 1, :] = jnp.sum(fold_lanes(jnp.add, block * block).T, axis=0, keepdims=True)
    bias_far.wait_recv()
    bias_pass = send(far_bias, far_bias, 4 * PIECES + 3, sibling)

    def pass_on(piece):
        up[piece].wait_recv()
        down[piece].wait_recv()
        land = far_t.at[piece, pl.ds(pl.multiple_of(core * 2 * PART, 2 * PART), 2 * PART)]
        return send(land, land, 4 * piece + 2, sibling)

    passed = pass_on(0)

    @pl.when(core == 1)
    def _():
        news(2, 2)
        news(3, 1)
        tell(4, [sibling])
        tell(5, y_sides)

    bias_pass.wait_recv()
    widen(2)
    widen(3)
    for piece in range(PIECES):
        segments = [
            pl.ds(2 * BLOCK + of_core * BLOCK + half * (BLOCK // 2) + piece * PART, PART)
            for of_core in range(2)
            for half in range(2)
        ]
        passed.wait_recv()
        if piece + 1 < PIECES:
            row_pass(far_t.at[piece], segments, range(1))
            passed = pass_on(piece + 1)

            @pl.when(core == 1)
            def _():
                news(5, 2)
                tell(6, [plane(SIDE // 2, 1)])

            row_pass(far_t.at[piece], segments, range(1, 4))
        else:
            row_pass(far_t.at[piece], segments, range(4))

    peak, total = row_max[...], row_sum[...]
    top = jnp.max(peak, axis=0, keepdims=True)
    row_log = top + jnp.log2(jnp.sum(total * jnp.exp2(peak - top), axis=0, keepdims=True))
    shift[...] = shift[...] - row_log
    row_max[0:1, :] = row_log

    def reduce_send(from_ref, to_ref, stage, peer):
        copy = pltpu.make_async_remote_copy(
            src_ref=from_ref,
            dst_ref=to_ref,
            send_sem=reduce_sem.at[2 * stage],
            recv_sem=reduce_sem.at[2 * stage + 1],
            device_id=peer,
            device_id_type=MESH,
        )
        copy.start()
        return copy

    def arrived(ref, stage):
        pltpu.make_async_copy(ref, ref, reduce_sem.at[2 * stage + 1]).wait()

    def left(ref, stage):
        pltpu.make_async_copy(ref, ref, reduce_sem.at[2 * stage]).wait()

    def merge(value, rows):
        deep = value.reshape(-1, 8, TILE)
        peak = jnp.max(deep, axis=0)
        total = jnp.sum(jnp.exp2(deep - peak[None]), axis=0)
        parts = [slice(n, n + rows) for n in range(0, 8, rows)]
        top = functools.reduce(jnp.maximum, [peak[p] for p in parts])
        return top + jnp.log2(sum(total[p] * jnp.exp2(peak[p] - top) for p in parts))

    def column_pass(blocks):
        for block in blocks:
            for group in range(TILE // 8):
                rows = pl.ds(block * TILE + group * 8, 8)
                value = scores[rows, :] + shift[...]
                peak = fold_lanes(jnp.maximum, value)
                deep = jnp.concatenate([peak] * (ROWS // TILE), axis=1)
                col_max[rows, :] = peak
                col_sum[rows, :] = fold_lanes(jnp.add, jnp.exp2(value - deep))
            rows = pl.ds(block * TILE, TILE)
            peaks = col_max[rows, :].T
            peak = jnp.max(peaks, axis=0, keepdims=True)
            total = jnp.sum(col_sum[rows, :].T * jnp.exp2(peaks - peak), axis=0, keepdims=True)
            col_log[block : block + 1, :] = peak + jnp.log2(total)

    @pl.when(core == 0)
    def _():
        news(4, 1)

    for parity in range(2):
        column_pass(range(4 * parity, 4 * parity + 4))
        for step in line_steps:
            if step % 2 == parity:
                slot = pl.ds(pl.multiple_of(8 * step + 4 * core, 4), 4)
                reduce_send(col_log.at[4 * parity : 4 * parity + 4], line_in.at[slot], 0, line(step, 1))

    @pl.when(core == 0)
    def _():
        reduce_send(col_log.at[0:4], line_in.at[0:4], 0, sibling)

    for tile in range(ROWS // TILE):
        lanes = pl.ds(tile * TILE, TILE)
        src_out[lanes] = (
            norms[tile : tile + 1, :] / 32.0 - 64.0 - (0.5 * LN2) * row_max[0:1, lanes]
        ).reshape(TILE)

    @pl.when(core == 0)
    def _():
        arrived(plane_in, 1)
        left(line_in.at[0:32], 0)

    @pl.when(core == 1)
    def _():
        line_in[4:8, :] = col_log[0:4, :]
        arrived(line_in.at[0:60], 0)
        line_out[0:4, :] = merge(line_in[...], 4)
        news(6, 1)
        for step in plane_steps:
            for to in range(2):
                reduce_send(
                    line_out.at[2 * to : 2 * to + 2], plane_in.at[2 * step : 2 * step + 2], 1, plane(step, to)
                )
        reduce_send(line_out.at[0:2], plane_in.at[0:2], 1, sibling)
        plane_in[0:2, :] = line_out[2:4, :]
        arrived(plane_in.at[2:32], 1)
        left(line_in.at[0:28], 0)
        left(line_in.at[0:62], 1)

    tgt_new = bias_v[0:2, :] + 0.5 * bias_v[8:10, :] - (0.5 * LN2) * merge(plane_in[...], 2)
    for half in range(2):
        tgt_out[half * TILE : (half + 1) * TILE] = tgt_new[half : half + 1, :].reshape(TILE)

    for copy in sends:
        copy.wait_send()


def finish(src_in, tgt_in, src_out, tgt_out, sem):
    one = pltpu.make_async_copy(src_in, src_out, sem.at[0])
    two = pltpu.make_async_copy(tgt_in, tgt_out, sem.at[1])
    one.start()
    two.start()
    one.wait()
    two.wait()


def local(sources, targets, log_src, log_tgt, potential):
    anywhere = pl.BlockSpec(memory_space=pl.ANY)
    vmem = pl.BlockSpec(memory_space=pltpu.VMEM)
    src_out, tgt_out = pl.pallas_call(
        kernel,
        out_shape=[
            pltpu.VMEM((ROWS,), F32),
            pltpu.VMEM((BLOCK,), F32),
        ],
        in_specs=[anywhere] * 5,
        out_specs=[vmem] * 2,
        scratch_shapes=[
            pltpu.VMEM((ROWS, WIDTH), jnp.bfloat16),
            pltpu.VMEM((2 * BLOCK, WIDTH), jnp.bfloat16),
            pltpu.VMEM((PIECES, 4 * PART, WIDTH), jnp.bfloat16),
            pltpu.VMEM((16, TILE), F32),
            pltpu.VMEM((ROWS // TILE, TILE), F32),
            pltpu.VMEM((8, TILE), F32),
            pltpu.VMEM((COLS, TILE), F32),
            pltpu.VMEM((ROWS // TILE, TILE), F32),
            pltpu.VMEM((COLS, ROWS), F32),
            pltpu.VMEM((8, ROWS), F32),
            pltpu.VMEM((8, ROWS), F32),
            pltpu.VMEM((8, ROWS), F32),
            pltpu.VMEM((COLS, TILE), F32),
            pltpu.VMEM((COLS, TILE), F32),
            pltpu.VMEM((8, TILE), F32),
            pltpu.VMEM((64, TILE), F32),
            pltpu.VMEM((8, TILE), F32),
            pltpu.VMEM((32, TILE), F32),
            pltpu.SemaphoreType.DMA((8,)),
            pltpu.SemaphoreType.DMA((4 * PIECES + 4,)),
            pltpu.SemaphoreType.DMA((4 * PIECES + 4,)),
            pltpu.SemaphoreType.DMA((4,)),
            pltpu.SemaphoreType.REGULAR((7,)),
        ],
        compiler_params=pltpu.CompilerParams(
            collective_id=0, has_side_effects=True, vmem_limit_bytes=56 * 2**20
        ),
        cost_estimate=pl.CostEstimate(
            flops=2 * ROWS * COLS * WIDTH,
            bytes_accessed=2 * WIDTH * (ROWS + COLS),
            transcendentals=2 * ROWS * COLS,
        ),
    )(
        sources,
        targets,
        log_src.reshape(ROWS // TILE, TILE),
        log_tgt.reshape(BLOCK // TILE, TILE),
        potential.reshape(BLOCK // TILE, TILE),
    )
    return pl.pallas_call(
        finish,
        out_shape=[jax.ShapeDtypeStruct((ROWS,), F32), jax.ShapeDtypeStruct((BLOCK,), F32)],
        in_specs=[vmem] * 2,
        out_specs=[anywhere] * 2,
        scratch_shapes=[pltpu.SemaphoreType.DMA((2,))],
    )(
        pltpu.with_memory_space_constraint(src_out, pltpu.VMEM),
        pltpu.with_memory_space_constraint(tgt_out, pltpu.VMEM),
    )


def solution(mesh):
    placed = (P(("src", "blk"), None), P("blk", None), P(("src", "blk")), P("blk"), P("blk"))
    return jax.shard_map(
        local, mesh=mesh, in_specs=placed, out_specs=(P(("src", "blk")), P("blk")), check_vma=False
    )
```

```python
import functools
import math

import jax
import jax.numpy as jnp
from jax import lax
from jax.experimental import pallas as pl
from jax.experimental.pallas import tpu as pltpu
from jax.sharding import PartitionSpec as P

MESH = pl.DeviceIdType.MESH
LOG2E = math.log2(math.e)
LN2 = math.log(2.0)
F32 = jnp.float32

ROWS = 2048
COLS = 1024
BLOCK = 256
WIDTH = 1024
TILE = 128
SIDE = 4
PIECES = 2
PART = BLOCK // 2 // PIECES


def dot_t(left, right):
    return lax.dot_general(left, right, (((1,), (1,)), ((), ())), preferred_element_type=F32)


def fold_lanes(op, value):
    while value.shape[1] > TILE:
        half = value.shape[1] // 2
        value = op(value[:, :half], value[:, half:])
    return value


def line_hops(step):
    return min(step, 2 * SIDE - step)


def plane_hops(step):
    return sum(min(n, SIDE - n) for n in divmod(step, SIDE))


def kernel(
    sources,
    targets,
    log_src,
    log_tgt,
    potential,
    src_out,
    tgt_out,
    src_v,
    near_t,
    far_t,
    bias_v,
    weight_v,
    row_bias,
    wide_bias,
    norms,
    scores,
    row_max,
    row_sum,
    shift,
    col_max,
    col_sum,
    col_log,
    line_in,
    line_out,
    plane_in,
    load_sem,
    send_sem,
    recv_sem,
    reduce_sem,
    news_sem,
):
    src = lax.axis_index("src")
    blk = lax.axis_index("blk")
    x, y, z_hi = src // (SIDE * SIDE), (src // SIDE) % SIDE, src % SIDE
    z_lo, core = blk // 2, blk % 2
    z = z_hi * 2 + z_lo

    def device(to_x, to_y, to_z, to_core):
        return ((to_x * SIDE + to_y) * SIDE + to_z // 2, (to_z % 2) * 2 + to_core)

    def line(step, to_core):
        return device(x, y, (z + step) % (2 * SIDE), to_core)

    def plane(step, to_core):
        return device((x + step // SIDE) % SIDE, (y + step % SIDE) % SIDE, z, to_core)

    sibling = line(0, 1 - core)
    above, below = line(1, core), line(2 * SIDE - 1, core)

    loads = []

    def load(from_ref, to_ref):
        copy = pltpu.make_async_copy(from_ref, to_ref, load_sem.at[len(loads)])
        copy.start()
        loads.append(copy)
        return copy

    own_rows = pl.ds(pl.multiple_of(core * BLOCK, BLOCK), BLOCK)
    sib_rows = pl.ds(pl.multiple_of((1 - core) * BLOCK, BLOCK), BLOCK)
    load_t = load(targets, near_t.at[own_rows])
    load_p = load(potential, bias_v.at[0:2])
    load_l = load(log_tgt, bias_v.at[8:10])
    load_w = load(log_src, weight_v)
    quarter = ROWS // 4
    load_s = [
        load(sources.at[n * quarter : (n + 1) * quarter], src_v.at[n * quarter : (n + 1) * quarter])
        for n in range(4)
    ]

    barrier = pltpu.get_barrier_semaphore()
    line_steps = sorted(range(1, 2 * SIDE), key=line_hops, reverse=True)
    plane_steps = sorted(range(1, SIDE * SIDE), key=plane_hops, reverse=True)

    def greet(peers):
        for peer in peers:
            pl.semaphore_signal(barrier, inc=1, device_id=peer, device_id_type=MESH)

    x_sides = [plane(n * SIDE, 1) for n in (1, SIDE - 1)]
    y_sides = [plane(n, 1) for n in (1, SIDE - 1)]
    lone = [sibling, above, below]
    hub = lone + x_sides + y_sides

    @pl.when(core == 0)
    def _():
        greet(lone)

    @pl.when(core == 1)
    def _():
        greet(hub)

    sends = []

    def send(from_ref, to_ref, number, peer):
        copy = pltpu.make_async_remote_copy(
            src_ref=from_ref,
            dst_ref=to_ref,
            send_sem=send_sem.at[number],
            recv_sem=recv_sem.at[number],
            device_id=peer,
            device_id_type=MESH,
        )
        copy.start()
        sends.append(copy)
        return copy

    core_rows = core * BLOCK
    load_t.wait()
    load_p.wait()
    load_l.wait()
    for half in range(2):
        rows = pl.ds(pl.multiple_of(core_rows + half * TILE, TILE), TILE)
        block = near_t[rows, :].astype(F32)
        tgt_norms = jnp.sum(fold_lanes(jnp.add, block * block).T, axis=0, keepdims=True)
        bias = bias_v[8 + half : 9 + half, :] + 2.0 * bias_v[half : half + 1, :]
        row_bias[pl.ds(core * 2 + half, 1), :] = (bias - tgt_norms / 16.0) * LOG2E

    def widen(slot):
        for half in range(2):
            row = jnp.broadcast_to(row_bias[pl.ds(slot * 2 + half, 1), :], (TILE, TILE))
            wide_bias[pl.ds(pl.multiple_of(slot * BLOCK + half * TILE, TILE), TILE), :] = row.T

    widen(core)
    load_w.wait()
    weights = jnp.concatenate([weight_v[n : n + 1, :] for n in range(ROWS // TILE)], axis=1)
    shift[...] = jnp.broadcast_to(weights * LOG2E, (8, ROWS))

    @pl.when(core == 0)
    def _():
        pl.semaphore_wait(barrier, len(lone))

    @pl.when(core == 1)
    def _():
        pl.semaphore_wait(barrier, len(hub))

    up, down = [], []
    own_bias = row_bias.at[pl.ds(core * 2, 2)]
    far_bias = row_bias.at[pl.ds(4 + core * 2, 2)]
    bias_far = send(own_bias, far_bias, 4 * PIECES + 2, above)
    bias_near = send(own_bias, own_bias, 4 * PIECES + 1, sibling)
    near = send(near_t.at[own_rows], near_t.at[own_rows], 4 * PIECES, sibling)
    for piece in range(PIECES):
        low = pl.ds(pl.multiple_of(core_rows + piece * PART, PART), PART)
        high = pl.ds(pl.multiple_of(core_rows + BLOCK // 2 + piece * PART, PART), PART)
        land_low = pl.ds(pl.multiple_of(core * 2 * PART, PART), PART)
        land_high = pl.ds(pl.multiple_of(core * 2 * PART + PART, PART), PART)
        up.append(send(near_t.at[low], far_t.at[piece, land_low], 4 * piece, above))
        down.append(send(near_t.at[high], far_t.at[piece, land_high], 4 * piece + 1, below))
    own_bias = row_bias.at[pl.ds(core * 2, 2)]
    far_bias = row_bias.at[pl.ds(4 + core * 2, 2)]

    def news(number, amount):
        pl.semaphore_wait(news_sem.at[number], amount)

    def tell(number, peers):
        for peer in peers:
            pl.semaphore_signal(news_sem.at[number], inc=1, device_id=peer, device_id_type=MESH)

    @pl.when(core == 1)
    def _():
        tell(0, [above, below])
        tell(1, x_sides)

    def row_pass(moving, segments, parts, waits=()):
        length = moving.shape[0] // len(segments)
        for part in parts:
            if waits:
                waits[part].wait()
            bias = [wide_bias[rows, :] for rows in segments]
            bias = bias[0] if len(bias) == 1 else jnp.concatenate(bias, axis=0)
            inner = dot_t(moving[...], src_v[part * quarter : (part + 1) * quarter, :])
            for tile in range(quarter // TILE):
                lanes = pl.ds(part * quarter + tile * TILE, TILE)
                value = inner[:, tile * TILE : (tile + 1) * TILE] * (LOG2E / 8.0) + bias
                for at, rows in enumerate(segments):
                    scores[rows, lanes] = value[at * length : (at + 1) * length, :]
                deep = value.reshape(-1, 8, TILE)
                top = jnp.max(deep, axis=0)
                if waits:
                    row_sum[:, lanes] = jnp.sum(jnp.exp2(deep - top[None]), axis=0)
                else:
                    before = row_max[:, lanes]
                    top = jnp.maximum(top, before)
                    row_sum[:, lanes] = row_sum[:, lanes] * jnp.exp2(before - top) + jnp.sum(
                        jnp.exp2(deep - top[None]), axis=0
                    )
                row_max[:, lanes] = top

    row_pass(near_t.at[own_rows], [own_rows], range(4), load_s)
    near.wait_recv()
    bias_near.wait_recv()
    widen(1 - core)
    row_pass(near_t.at[sib_rows], [sib_rows], range(4))

    @pl.when(core == 1)
    def _():
        news(0, 2)
        news(1, 2)
        tell(2, [line(2, 1), line(2 * SIDE - 2, 1)])
        tell(3, [plane(2 * SIDE, 1)])

    bias_far.wait_recv()
    bias_pass = send(far_bias, far_bias, 4 * PIECES + 3, sibling)

    def pass_on(piece):
        up[piece].wait_recv()
        down[piece].wait_recv()
        land = far_t.at[piece, pl.ds(pl.multiple_of(core * 2 * PART, 2 * PART), 2 * PART)]
        return send(land, land, 4 * piece + 2, sibling)

    passed = pass_on(0)

    @pl.when(core == 1)
    def _():
        news(2, 2)
        news(3, 1)
        tell(4, [sibling])
        tell(5, y_sides)

    bias_pass.wait_recv()
    widen(2)
    widen(3)
    for piece in range(PIECES):
        segments = [
            pl.ds(2 * BLOCK + of_core * BLOCK + half * (BLOCK // 2) + piece * PART, PART)
            for of_core in range(2)
            for half in range(2)
        ]
        passed.wait_recv()
        if piece + 1 < PIECES:
            row_pass(far_t.at[piece], segments, range(1))
            passed = pass_on(piece + 1)

            @pl.when(core == 1)
            def _():
                news(5, 2)
                tell(6, [plane(SIDE // 2, 1)])

            row_pass(far_t.at[piece], segments, range(1, 4))
        else:
            row_pass(far_t.at[piece], segments, range(4))

    peak, total = row_max[...], row_sum[...]
    top = jnp.max(peak, axis=0, keepdims=True)
    row_log = top + jnp.log2(jnp.sum(total * jnp.exp2(peak - top), axis=0, keepdims=True))
    shift[...] = shift[...] - row_log
    row_max[0:1, :] = row_log

    def reduce_send(from_ref, to_ref, stage, peer):
        copy = pltpu.make_async_remote_copy(
            src_ref=from_ref,
            dst_ref=to_ref,
            send_sem=reduce_sem.at[2 * stage],
            recv_sem=reduce_sem.at[2 * stage + 1],
            device_id=peer,
            device_id_type=MESH,
        )
        copy.start()
        return copy

    def arrived(ref, stage):
        pltpu.make_async_copy(ref, ref, reduce_sem.at[2 * stage + 1]).wait()

    def left(ref, stage):
        pltpu.make_async_copy(ref, ref, reduce_sem.at[2 * stage]).wait()

    def merge(value, rows):
        deep = value.reshape(-1, 8, TILE)
        peak = jnp.max(deep, axis=0)
        total = jnp.sum(jnp.exp2(deep - peak[None]), axis=0)
        parts = [slice(n, n + rows) for n in range(0, 8, rows)]
        top = functools.reduce(jnp.maximum, [peak[p] for p in parts])
        return top + jnp.log2(sum(total[p] * jnp.exp2(peak[p] - top) for p in parts))

    def column_pass(blocks):
        for block in blocks:
            for group in range(TILE // 8):
                rows = pl.ds(block * TILE + group * 8, 8)
                value = scores[rows, :] + shift[...]
                peak = fold_lanes(jnp.maximum, value)
                deep = jnp.concatenate([peak] * (ROWS // TILE), axis=1)
                col_max[rows, :] = peak
                col_sum[rows, :] = fold_lanes(jnp.add, jnp.exp2(value - deep))
            rows = pl.ds(block * TILE, TILE)
            peaks = col_max[rows, :].T
            peak = jnp.max(peaks, axis=0, keepdims=True)
            total = jnp.sum(col_sum[rows, :].T * jnp.exp2(peaks - peak), axis=0, keepdims=True)
            col_log[block : block + 1, :] = peak + jnp.log2(total)

    @pl.when(core == 0)
    def _():
        news(4, 1)

    for parity in range(2):
        column_pass(range(4 * parity, 4 * parity + 4))
        for step in line_steps:
            if step % 2 == parity:
                slot = pl.ds(pl.multiple_of(8 * step + 4 * core, 4), 4)
                reduce_send(col_log.at[4 * parity : 4 * parity + 4], line_in.at[slot], 0, line(step, 1))

    @pl.when(core == 0)
    def _():
        reduce_send(col_log.at[0:4], line_in.at[0:4], 0, sibling)

    for tile in range(ROWS // TILE):
        block = src_v[tile * TILE : (tile + 1) * TILE, :].astype(F32)
        norms[tile : tile + 1, :] = jnp.sum(fold_lanes(jnp.add, block * block).T, axis=0, keepdims=True)
    for tile in range(ROWS // TILE):
        lanes = pl.ds(tile * TILE, TILE)
        src_out[lanes] = (
            norms[tile : tile + 1, :] / 32.0 - 64.0 - (0.5 * LN2) * row_max[0:1, lanes]
        ).reshape(TILE)

    @pl.when(core == 0)
    def _():
        arrived(plane_in, 1)

    @pl.when(core == 1)
    def _():
        line_in[4:8, :] = col_log[0:4, :]
        arrived(line_in.at[0:60], 0)
        line_out[0:4, :] = merge(line_in[...], 4)
        news(6, 1)
        for to in (1, 0):
            for step in plane_steps:
                reduce_send(
                    line_out.at[2 * to : 2 * to + 2], plane_in.at[2 * step : 2 * step + 2], 1, plane(step, to)
                )
        reduce_send(line_out.at[0:2], plane_in.at[0:2], 1, sibling)
        plane_in[0:2, :] = line_out[2:4, :]
        arrived(plane_in.at[2:32], 1)

    tgt_new = bias_v[0:2, :] + 0.5 * bias_v[8:10, :] - (0.5 * LN2) * merge(plane_in[...], 2)
    for half in range(2):
        tgt_out[half * TILE : (half + 1) * TILE] = tgt_new[half : half + 1, :].reshape(TILE)

    for copy in sends:
        copy.wait_send()

    @pl.when(core == 0)
    def _():
        left(line_in.at[0:32], 0)

    @pl.when(core == 1)
    def _():
        left(line_in.at[0:28], 0)
        left(line_in.at[0:62], 1)


def finish(src_in, tgt_in, src_out, tgt_out, sem):
    one = pltpu.make_async_copy(src_in, src_out, sem.at[0])
    two = pltpu.make_async_copy(tgt_in, tgt_out, sem.at[1])
    one.start()
    two.start()
    one.wait()
    two.wait()


def local(sources, targets, log_src, log_tgt, potential):
    anywhere = pl.BlockSpec(memory_space=pl.ANY)
    vmem = pl.BlockSpec(memory_space=pltpu.VMEM)
    src_out, tgt_out = pl.pallas_call(
        kernel,
        out_shape=[
            pltpu.VMEM((ROWS,), F32),
            pltpu.VMEM((BLOCK,), F32),
        ],
        in_specs=[anywhere] * 5,
        out_specs=[vmem] * 2,
        scratch_shapes=[
            pltpu.VMEM((ROWS, WIDTH), jnp.bfloat16),
            pltpu.VMEM((2 * BLOCK, WIDTH), jnp.bfloat16),
            pltpu.VMEM((PIECES, 4 * PART, WIDTH), jnp.bfloat16),
            pltpu.VMEM((16, TILE), F32),
            pltpu.VMEM((ROWS // TILE, TILE), F32),
            pltpu.VMEM((8, TILE), F32),
            pltpu.VMEM((COLS, TILE), F32),
            pltpu.VMEM((ROWS // TILE, TILE), F32),
            pltpu.VMEM((COLS, ROWS), F32),
            pltpu.VMEM((8, ROWS), F32),
            pltpu.VMEM((8, ROWS), F32),
            pltpu.VMEM((8, ROWS), F32),
            pltpu.VMEM((COLS, TILE), F32),
            pltpu.VMEM((COLS, TILE), F32),
            pltpu.VMEM((8, TILE), F32),
            pltpu.VMEM((64, TILE), F32),
            pltpu.VMEM((8, TILE), F32),
            pltpu.VMEM((32, TILE), F32),
            pltpu.SemaphoreType.DMA((8,)),
            pltpu.SemaphoreType.DMA((4 * PIECES + 4,)),
            pltpu.SemaphoreType.DMA((4 * PIECES + 4,)),
            pltpu.SemaphoreType.DMA((4,)),
            pltpu.SemaphoreType.REGULAR((7,)),
        ],
        compiler_params=pltpu.CompilerParams(
            collective_id=0, has_side_effects=True, vmem_limit_bytes=56 * 2**20
        ),
        cost_estimate=pl.CostEstimate(
            flops=2 * ROWS * COLS * WIDTH,
            bytes_accessed=2 * WIDTH * (ROWS + COLS),
            transcendentals=2 * ROWS * COLS,
        ),
    )(
        sources,
        targets,
        log_src.reshape(ROWS // TILE, TILE),
        log_tgt.reshape(BLOCK // TILE, TILE),
        potential.reshape(BLOCK // TILE, TILE),
    )
    return pl.pallas_call(
        finish,
        out_shape=[jax.ShapeDtypeStruct((ROWS,), F32), jax.ShapeDtypeStruct((BLOCK,), F32)],
        in_specs=[vmem] * 2,
        out_specs=[anywhere] * 2,
        scratch_shapes=[pltpu.SemaphoreType.DMA((2,))],
    )(
        pltpu.with_memory_space_constraint(src_out, pltpu.VMEM),
        pltpu.with_memory_space_constraint(tgt_out, pltpu.VMEM),
    )


def solution(mesh):
    placed = (P(("src", "blk"), None), P("blk", None), P(("src", "blk")), P("blk"), P("blk"))
    return jax.shard_map(
        local, mesh=mesh, in_specs=placed, out_specs=(P(("src", "blk")), P("blk")), check_vma=False
    )
```

```python
import functools
import math

import jax
import jax.numpy as jnp
from jax import lax
from jax.experimental import pallas as pl
from jax.experimental.pallas import tpu as pltpu
from jax.sharding import PartitionSpec as P

MESH = pl.DeviceIdType.MESH
LOG2E = math.log2(math.e)
LN2 = math.log(2.0)
F32 = jnp.float32

ROWS = 2048
COLS = 1024
BLOCK = 256
WIDTH = 1024
TILE = 128
SIDE = 4
PIECES = 2
PART = BLOCK // 2 // PIECES


def dot_t(left, right):
    return lax.dot_general(left, right, (((1,), (1,)), ((), ())), preferred_element_type=F32)


def fold_lanes(op, value):
    while value.shape[1] > TILE:
        half = value.shape[1] // 2
        value = op(value[:, :half], value[:, half:])
    return value


def line_hops(step):
    return min(step, 2 * SIDE - step)


def plane_hops(step):
    return sum(min(n, SIDE - n) for n in divmod(step, SIDE))


def kernel(
    sources,
    targets,
    log_src,
    log_tgt,
    potential,
    src_out,
    tgt_out,
    src_v,
    near_t,
    far_t,
    bias_v,
    weight_v,
    row_bias,
    wide_bias,
    norms,
    scores,
    row_max,
    row_sum,
    shift,
    col_max,
    col_sum,
    col_log,
    line_in,
    line_out,
    plane_in,
    load_sem,
    send_sem,
    recv_sem,
    reduce_sem,
    news_sem,
):
    src = lax.axis_index("src")
    blk = lax.axis_index("blk")
    x, y, z_hi = src // (SIDE * SIDE), (src // SIDE) % SIDE, src % SIDE
    z_lo, core = blk // 2, blk % 2
    z = z_hi * 2 + z_lo

    def device(to_x, to_y, to_z, to_core):
        return ((to_x * SIDE + to_y) * SIDE + to_z // 2, (to_z % 2) * 2 + to_core)

    def line(step, to_core):
        return device(x, y, (z + step) % (2 * SIDE), to_core)

    def plane(step, to_core):
        return device((x + step // SIDE) % SIDE, (y + step % SIDE) % SIDE, z, to_core)

    sibling = line(0, 1 - core)
    above, below = line(1, core), line(2 * SIDE - 1, core)

    loads = []

    def load(from_ref, to_ref):
        copy = pltpu.make_async_copy(from_ref, to_ref, load_sem.at[len(loads)])
        copy.start()
        loads.append(copy)
        return copy

    own_rows = pl.ds(pl.multiple_of(core * BLOCK, BLOCK), BLOCK)
    sib_rows = pl.ds(pl.multiple_of((1 - core) * BLOCK, BLOCK), BLOCK)
    load_t = load(targets, near_t.at[own_rows])
    load_p = load(potential, bias_v.at[0:2])
    load_l = load(log_tgt, bias_v.at[8:10])
    load_w = load(log_src, weight_v)
    quarter = ROWS // 4
    load_s = [
        load(sources.at[n * quarter : (n + 1) * quarter], src_v.at[n * quarter : (n + 1) * quarter])
        for n in range(4)
    ]

    barrier = pltpu.get_barrier_semaphore()
    line_steps = sorted(range(1, 2 * SIDE), key=line_hops, reverse=True)
    plane_steps = sorted(range(1, SIDE * SIDE), key=plane_hops, reverse=True)

    def greet(peers):
        for peer in peers:
            pl.semaphore_signal(barrier, inc=1, device_id=peer, device_id_type=MESH)

    x_sides = [plane(n * SIDE, 1) for n in (1, SIDE - 1)]
    y_sides = [plane(n, 1) for n in (1, SIDE - 1)]
    lone = [sibling, above, below]
    hub = lone + x_sides + y_sides

    @pl.when(core == 0)
    def _():
        greet(lone)

    @pl.when(core == 1)
    def _():
        greet(hub)

    sends = []

    def send(from_ref, to_ref, number, peer):
        copy = pltpu.make_async_remote_copy(
            src_ref=from_ref,
            dst_ref=to_ref,
            send_sem=send_sem.at[number],
            recv_sem=recv_sem.at[number],
            device_id=peer,
            device_id_type=MESH,
        )
        copy.start()
        sends.append(copy)
        return copy

    core_rows = core * BLOCK
    load_t.wait()
    load_p.wait()
    load_l.wait()
    for half in range(2):
        rows = pl.ds(pl.multiple_of(core_rows + half * TILE, TILE), TILE)
        block = near_t[rows, :].astype(F32)
        tgt_norms = jnp.sum(fold_lanes(jnp.add, block * block).T, axis=0, keepdims=True)
        bias = bias_v[8 + half : 9 + half, :] + 2.0 * bias_v[half : half + 1, :]
        row_bias[pl.ds(core * 2 + half, 1), :] = (bias - tgt_norms / 16.0) * LOG2E

    def widen(slot):
        for half in range(2):
            row = jnp.broadcast_to(row_bias[pl.ds(slot * 2 + half, 1), :], (TILE, TILE))
            wide_bias[pl.ds(pl.multiple_of(slot * BLOCK + half * TILE, TILE), TILE), :] = row.T

    widen(core)
    load_w.wait()
    weights = jnp.concatenate([weight_v[n : n + 1, :] for n in range(ROWS // TILE)], axis=1)
    shift[...] = jnp.broadcast_to(weights * LOG2E, (8, ROWS))

    @pl.when(core == 0)
    def _():
        pl.semaphore_wait(barrier, len(lone))

    @pl.when(core == 1)
    def _():
        pl.semaphore_wait(barrier, len(hub))

    up, down = [], []
    own_bias = row_bias.at[pl.ds(core * 2, 2)]
    far_bias = row_bias.at[pl.ds(4 + core * 2, 2)]
    bias_far = send(own_bias, far_bias, 4 * PIECES + 2, above)
    bias_near = send(own_bias, own_bias, 4 * PIECES + 1, sibling)
    near = send(near_t.at[own_rows], near_t.at[own_rows], 4 * PIECES, sibling)
    for piece in range(PIECES):
        low = pl.ds(pl.multiple_of(core_rows + piece * PART, PART), PART)
        high = pl.ds(pl.multiple_of(core_rows + BLOCK // 2 + piece * PART, PART), PART)
        land_low = pl.ds(pl.multiple_of(core * 2 * PART, PART), PART)
        land_high = pl.ds(pl.multiple_of(core * 2 * PART + PART, PART), PART)
        up.append(send(near_t.at[low], far_t.at[piece, land_low], 4 * piece, above))
        down.append(send(near_t.at[high], far_t.at[piece, land_high], 4 * piece + 1, below))
    own_bias = row_bias.at[pl.ds(core * 2, 2)]
    far_bias = row_bias.at[pl.ds(4 + core * 2, 2)]

    def news(number, amount):
        pl.semaphore_wait(news_sem.at[number], amount)

    def tell(number, peers):
        for peer in peers:
            pl.semaphore_signal(news_sem.at[number], inc=1, device_id=peer, device_id_type=MESH)

    @pl.when(core == 1)
    def _():
        tell(0, [above, below])
        tell(1, x_sides)

    def row_pass(moving, segments, parts, waits=()):
        length = moving.shape[0] // len(segments)
        for part in parts:
            if waits:
                waits[part].wait()
            bias = [wide_bias[rows, :] for rows in segments]
            bias = bias[0] if len(bias) == 1 else jnp.concatenate(bias, axis=0)
            inner = dot_t(moving[...], src_v[part * quarter : (part + 1) * quarter, :])
            for tile in range(quarter // TILE):
                lanes = pl.ds(part * quarter + tile * TILE, TILE)
                value = inner[:, tile * TILE : (tile + 1) * TILE] * (LOG2E / 8.0) + bias
                for at, rows in enumerate(segments):
                    scores[rows, lanes] = value[at * length : (at + 1) * length, :]
                deep = value.reshape(-1, 8, TILE)
                top = jnp.max(deep, axis=0)
                if waits:
                    row_sum[:, lanes] = jnp.sum(jnp.exp2(deep - top[None]), axis=0)
                else:
                    before = row_max[:, lanes]
                    top = jnp.maximum(top, before)
                    row_sum[:, lanes] = row_sum[:, lanes] * jnp.exp2(before - top) + jnp.sum(
                        jnp.exp2(deep - top[None]), axis=0
                    )
                row_max[:, lanes] = top

    row_pass(near_t.at[own_rows], [own_rows], range(4), load_s)
    near.wait_recv()
    bias_near.wait_recv()
    widen(1 - core)
    row_pass(near_t.at[sib_rows], [sib_rows], range(4))

    @pl.when(core == 1)
    def _():
        news(0, 2)
        news(1, 2)
        tell(2, [line(2, 1), line(2 * SIDE - 2, 1)])
        tell(3, [plane(2 * SIDE, 1)])

    bias_far.wait_recv()
    bias_pass = send(far_bias, far_bias, 4 * PIECES + 3, sibling)

    def pass_on(piece):
        up[piece].wait_recv()
        down[piece].wait_recv()
        land = far_t.at[piece, pl.ds(pl.multiple_of(core * 2 * PART, 2 * PART), 2 * PART)]
        return send(land, land, 4 * piece + 2, sibling)

    passed = pass_on(0)

    @pl.when(core == 1)
    def _():
        news(2, 2)
        news(3, 1)
        tell(4, [sibling])
        tell(5, y_sides)

    bias_pass.wait_recv()
    widen(2)
    widen(3)
    for piece in range(PIECES):
        segments = [
            pl.ds(2 * BLOCK + of_core * BLOCK + half * (BLOCK // 2) + piece * PART, PART)
            for of_core in range(2)
            for half in range(2)
        ]
        passed.wait_recv()
        if piece + 1 < PIECES:
            row_pass(far_t.at[piece], segments, range(1))
            passed = pass_on(piece + 1)

            @pl.when(core == 1)
            def _():
                news(5, 2)
                tell(6, [plane(SIDE // 2, 1)])

            row_pass(far_t.at[piece], segments, range(1, 4))
        else:
            row_pass(far_t.at[piece], segments, range(4))

    peak, total = row_max[...], row_sum[...]
    top = jnp.max(peak, axis=0, keepdims=True)
    row_log = top + jnp.log2(jnp.sum(total * jnp.exp2(peak - top), axis=0, keepdims=True))
    shift[...] = shift[...] - row_log
    row_max[0:1, :] = row_log

    def reduce_send(from_ref, to_ref, stage, peer):
        copy = pltpu.make_async_remote_copy(
            src_ref=from_ref,
            dst_ref=to_ref,
            send_sem=reduce_sem.at[2 * stage],
            recv_sem=reduce_sem.at[2 * stage + 1],
            device_id=peer,
            device_id_type=MESH,
        )
        copy.start()
        return copy

    def arrived(ref, stage):
        pltpu.make_async_copy(ref, ref, reduce_sem.at[2 * stage + 1]).wait()

    def left(ref, stage):
        pltpu.make_async_copy(ref, ref, reduce_sem.at[2 * stage]).wait()

    def merge(value, rows):
        deep = value.reshape(-1, 8, TILE)
        peak = jnp.max(deep, axis=0)
        total = jnp.sum(jnp.exp2(deep - peak[None]), axis=0)
        parts = [slice(n, n + rows) for n in range(0, 8, rows)]
        top = functools.reduce(jnp.maximum, [peak[p] for p in parts])
        return top + jnp.log2(sum(total[p] * jnp.exp2(peak[p] - top) for p in parts))

    def column_pass(blocks):
        for block in blocks:
            for group in range(TILE // 8):
                rows = pl.ds(block * TILE + group * 8, 8)
                value = scores[rows, :] + shift[...]
                peak = fold_lanes(jnp.maximum, value)
                deep = jnp.concatenate([peak] * (ROWS // TILE), axis=1)
                col_max[rows, :] = peak
                col_sum[rows, :] = fold_lanes(jnp.add, jnp.exp2(value - deep))
            rows = pl.ds(block * TILE, TILE)
            peaks = col_max[rows, :].T
            peak = jnp.max(peaks, axis=0, keepdims=True)
            total = jnp.sum(col_sum[rows, :].T * jnp.exp2(peaks - peak), axis=0, keepdims=True)
            col_log[block : block + 1, :] = peak + jnp.log2(total)

    @pl.when(core == 0)
    def _():
        news(4, 1)

    for parity in range(2):
        column_pass(range(4 * parity, 4 * parity + 4))
        for step in line_steps:
            if step % 2 == parity:
                slot = pl.ds(pl.multiple_of(8 * step + 4 * core, 4), 4)
                reduce_send(col_log.at[4 * parity : 4 * parity + 4], line_in.at[slot], 0, line(step, 1))

    @pl.when(core == 0)
    def _():
        reduce_send(col_log.at[0:4], line_in.at[0:4], 0, sibling)

    def source_result():
        for tile in range(ROWS // TILE):
            block = src_v[tile * TILE : (tile + 1) * TILE, :].astype(F32)
            norms[tile : tile + 1, :] = jnp.sum(fold_lanes(jnp.add, block * block).T, axis=0, keepdims=True)
        for tile in range(ROWS // TILE):
            lanes = pl.ds(tile * TILE, TILE)
            src_out[lanes] = (
                norms[tile : tile + 1, :] / 32.0 - 64.0 - (0.5 * LN2) * row_max[0:1, lanes]
            ).reshape(TILE)

    @pl.when(core == 0)
    def _():
        source_result()
        arrived(plane_in, 1)

    @pl.when(core == 1)
    def _():
        line_in[4:8, :] = col_log[0:4, :]
        arrived(line_in.at[0:60], 0)
        line_out[0:4, :] = merge(line_in[...], 4)
        news(6, 1)
        for to in (1, 0):
            for step in plane_steps:
                reduce_send(
                    line_out.at[2 * to : 2 * to + 2], plane_in.at[2 * step : 2 * step + 2], 1, plane(step, to)
                )
        reduce_send(line_out.at[0:2], plane_in.at[0:2], 1, sibling)
        plane_in[0:2, :] = line_out[2:4, :]
        source_result()
        arrived(plane_in.at[2:32], 1)

    tgt_new = bias_v[0:2, :] + 0.5 * bias_v[8:10, :] - (0.5 * LN2) * merge(plane_in[...], 2)
    for half in range(2):
        tgt_out[half * TILE : (half + 1) * TILE] = tgt_new[half : half + 1, :].reshape(TILE)

    for copy in sends:
        copy.wait_send()

    @pl.when(core == 0)
    def _():
        left(line_in.at[0:32], 0)

    @pl.when(core == 1)
    def _():
        left(line_in.at[0:28], 0)
        left(line_in.at[0:62], 1)


def finish(src_in, tgt_in, src_out, tgt_out, sem):
    one = pltpu.make_async_copy(src_in, src_out, sem.at[0])
    two = pltpu.make_async_copy(tgt_in, tgt_out, sem.at[1])
    one.start()
    two.start()
    one.wait()
    two.wait()


def local(sources, targets, log_src, log_tgt, potential):
    anywhere = pl.BlockSpec(memory_space=pl.ANY)
    vmem = pl.BlockSpec(memory_space=pltpu.VMEM)
    src_out, tgt_out = pl.pallas_call(
        kernel,
        out_shape=[
            pltpu.VMEM((ROWS,), F32),
            pltpu.VMEM((BLOCK,), F32),
        ],
        in_specs=[anywhere] * 5,
        out_specs=[vmem] * 2,
        scratch_shapes=[
            pltpu.VMEM((ROWS, WIDTH), jnp.bfloat16),
            pltpu.VMEM((2 * BLOCK, WIDTH), jnp.bfloat16),
            pltpu.VMEM((PIECES, 4 * PART, WIDTH), jnp.bfloat16),
            pltpu.VMEM((16, TILE), F32),
            pltpu.VMEM((ROWS // TILE, TILE), F32),
            pltpu.VMEM((8, TILE), F32),
            pltpu.VMEM((COLS, TILE), F32),
            pltpu.VMEM((ROWS // TILE, TILE), F32),
            pltpu.VMEM((COLS, ROWS), F32),
            pltpu.VMEM((8, ROWS), F32),
            pltpu.VMEM((8, ROWS), F32),
            pltpu.VMEM((8, ROWS), F32),
            pltpu.VMEM((COLS, TILE), F32),
            pltpu.VMEM((COLS, TILE), F32),
            pltpu.VMEM((8, TILE), F32),
            pltpu.VMEM((64, TILE), F32),
            pltpu.VMEM((8, TILE), F32),
            pltpu.VMEM((32, TILE), F32),
            pltpu.SemaphoreType.DMA((8,)),
            pltpu.SemaphoreType.DMA((4 * PIECES + 4,)),
            pltpu.SemaphoreType.DMA((4 * PIECES + 4,)),
            pltpu.SemaphoreType.DMA((4,)),
            pltpu.SemaphoreType.REGULAR((7,)),
        ],
        compiler_params=pltpu.CompilerParams(
            collective_id=0, has_side_effects=True, vmem_limit_bytes=56 * 2**20
        ),
        cost_estimate=pl.CostEstimate(
            flops=2 * ROWS * COLS * WIDTH,
            bytes_accessed=2 * WIDTH * (ROWS + COLS),
            transcendentals=2 * ROWS * COLS,
        ),
    )(
        sources,
        targets,
        log_src.reshape(ROWS // TILE, TILE),
        log_tgt.reshape(BLOCK // TILE, TILE),
        potential.reshape(BLOCK // TILE, TILE),
    )
    return pl.pallas_call(
        finish,
        out_shape=[jax.ShapeDtypeStruct((ROWS,), F32), jax.ShapeDtypeStruct((BLOCK,), F32)],
        in_specs=[vmem] * 2,
        out_specs=[anywhere] * 2,
        scratch_shapes=[pltpu.SemaphoreType.DMA((2,))],
    )(
        pltpu.with_memory_space_constraint(src_out, pltpu.VMEM),
        pltpu.with_memory_space_constraint(tgt_out, pltpu.VMEM),
    )


def solution(mesh):
    placed = (P(("src", "blk"), None), P("blk", None), P(("src", "blk")), P("blk"), P("blk"))
    return jax.shard_map(
        local, mesh=mesh, in_specs=placed, out_specs=(P(("src", "blk")), P("blk")), check_vma=False
    )
```
